32 devices in a mesh: req: 8 (over y, x, core), tp: 4 (over z).
Axes of the slice: x: 2, y: 2, z: 4, core: 2. Of those that a mesh axis runs over, the one named last changes fastest.
Arguments:
- hidden: bfloat16 [8, 384, 3584], P('req'), may hold values from -6 to 6
- embeds: bfloat16 [8, 384, 3584], P('req'), may hold values from -5 to 5
- lengths: int32 [8], P('req'), may hold values from 1 to 384, 1920 in all
- live: int32 [8], P('req'), may hold values 0 or 1
- adapter: int32 [8], P('req'), may hold values from 0 to 3
- incoming_mamba_state: float32 [8, 56, 64, 64], P('req', 'tp'), may hold values from -6 to 6
- mamba_norm_gain: float32 [3584], replicated, may hold values from 0.1 to 1.9
- trainer_gate_input_weight: float32 [3584, 2, 3584], P(('req', 'tp')), may hold values from -0.09375 to 0.09375
- trainer_step_weight: float32 [3584, 184], P(('req', 'tp')), may hold values from -0.09375 to 0.09375
- convolution_inner_taps: float32 [4, 3584], P(None, 'tp'), may hold values from -3 to 3
- convolution_bc_taps: float32 [4, 128], replicated, may hold values from -3 to 3
- step_bias: float32 [56], P('tp'), may hold values from -4 to -0.5
- head_decay_rate: float32 [56], P('tp'), may hold values from 0.05 to 1
- direct_head_term: float32 [56], P('tp'), may hold values from 0.5 to 1.5
- gated_norm_gain: float32 [3584], P('tp'), may hold values from 0.1 to 1.9
- trainer_mamba_output_weight: float32 [3584, 3584], P(None, ('req', 'tp')), may hold values from -0.09375 to 0.09375
- attention_norm_gain: float32 [7168], replicated, may hold values from 0.1 to 1.9
- trainer_query_key_value_weight: float32 [7168, 3, 3584], P(('req', 'tp')), may hold values from -0.33407655 to 0.33407655
- adapter_down_maps: bfloat16 [4, 7168, 128], replicated, may hold values from -0.0625 to 0.0625
- adapter_up_maps: bfloat16 [4, 128, 3, 3584], P(None, None, None, 'tp'), may hold values from -0.5 to 0.5
- trainer_output_weight: float32 [3584, 3584], P(None, ('req', 'tp')), may hold values from -0.09375 to 0.09375
Outputs:
- out_hidden: bfloat16 [8, 384, 3584], P('req', None, 'tp')
- out_state: float32 [8, 56, 64, 64], P('req', 'tp')
The draws below stay inside these ranges and needn't reach their ends.
Inputs may be any that keep to these rules, and one draw needn't show every extreme that they name: `lengths`: some request has length 384.
All inputs are finite; a program needn't handle non-finite values. No bound on the sum of `lengths` or of `live` on one device may be relied on, other than what follows from the above.
Results may differ from the reference program's by a relative error of at most 0.017.
Values may be sent and summed in bfloat16 or wider, within the bound.
No kernel may reach another device: no remote copies, remote signals or barrier semaphores. Data moves between devices by JAX's collectives and lax.ppermute only.
A program may use at most 384 MiB of HBM per device.

```python
import math
import jax
import jax.numpy as jnp
import numpy as np
from jax import lax

MODEL_WIDTH = 3584
MH = 56
P_SIZE = 64
NS = 64
CW = 4
HA = 16
HS = 224
ADAPTER_RANK = 128
ADAPTER_COUNT = 4
LEN = 384
SLOTS = 8
DI = 3584
ATTENTION_FEATS = 3584
N_TP = 4


def draw_embeds(key, part):
    base = jnp.clip(jax.random.normal(jax.random.fold_in(key, 11), (SLOTS, LEN, MODEL_WIDTH), jnp.float32), -5.0, 5.0)
    return base.astype(jnp.bfloat16)


def draw_trainer_query_key_value_weight(key, part):
    rows = 2 * MODEL_WIDTH
    base = jnp.clip(jax.random.normal(jax.random.fold_in(key, 21), (rows, 3, ATTENTION_FEATS), jnp.float32), -4.0, 4.0)
    drawn = base * float(rows) ** (-0.5)
    return drawn.astype(jnp.float32)


def plant(drawn, key, least, top_value):
    longest = drawn.shape.index(max(drawn.shape))
    spots = []
    for shift in (0, 1):
        where = [jax.random.randint(jax.random.fold_in(key, axis), (), 0, length) for axis, length in enumerate(drawn.shape)]
        where[longest] = (where[longest] + shift) % drawn.shape[longest]
        spots.append(tuple(where))
    return drawn.at[spots[0]].set(least).at[spots[1]].set(top_value)


def block_levels(rng, extent, shards, low, top_value):
    factor_of = 1.0
    for axis_at, blocks in shards:
        heights = jax.random.uniform(jax.random.fold_in(jax.random.fold_in(rng, 6), axis_at), (blocks,), jnp.float32, low / len(shards), top_value / len(shards))
        factor_of = factor_of * jnp.repeat(jnp.exp(heights), extent[axis_at] // blocks).reshape((-1,) + (1,) * (len(extent) - 1 - axis_at))
    return factor_of


def profile(amount, total, reach, lean):
    loads = [(1 << 20) // math.isqrt(grade ** lean) + 1 for grade in range(2, amount + 1)]
    rest, given = total - reach - (amount - 1), [1] * (amount - 1)
    while rest > 0:
        movable = [i for i in range(amount - 1) if given[i] < reach]
        mass, budget = sum([loads[i] for i in movable]), rest
        for i in movable:
            more = min(reach - given[i], max(1, budget * loads[i] // mass), rest)
            given[i] = given[i] + more
            rest = rest - more
    return np.array([reach] + given)


def uneven(rng, number_of, total, bound, skew):
    if number_of == 2:
        one = jax.random.randint(rng, (), max(1, total - bound), min(bound, total - 1) + 1)
        return jnp.stack([one, total - one])
    sizes = jnp.asarray(profile(number_of, total, bound, skew), jnp.int32)
    twos = (number_of - 1) // 2
    donor, taker = sizes[1:1 + 2 * twos:2], sizes[2:2 + 2 * twos:2]
    room = jnp.minimum(donor - 1, bound - taker)
    passed = jax.random.randint(jax.random.fold_in(rng, 1), (twos,), 0, 1 << 20) % (room + 1)
    sizes = sizes.at[1:1 + 2 * twos:2].set(donor - passed).at[2:2 + 2 * twos:2].set(taker + passed)
    return sizes[jax.random.permutation(jax.random.fold_in(rng, 2), number_of)]


def bell_draw(stream_key, extent, scale, limit, shards=(), kind=jnp.bfloat16):
    level = block_levels(stream_key, extent, shards, -0.22, 0.18) if shards else 1.0
    values = jax.random.normal(stream_key, extent, jnp.float32) * scale * level
    return jnp.minimum(jnp.maximum(values, -limit), limit).astype(kind)


def setup_inputs(seed: int = 0) -> dict:
    seeds = jax.random.split(jax.random.key(seed), 22)
    hidden = bell_draw(seeds[0], (SLOTS, LEN, MODEL_WIDTH), 1.0, 6.0, ((0, 8),))
    embeds = draw_embeds(jax.random.fold_in(seeds[21], 71), 0)
    lengths = uneven(seeds[2], SLOTS, SLOTS * LEN * 5 // 8, LEN, 2).astype(jnp.int32)
    live = plant((jax.random.randint(seeds[3], (SLOTS,), 0, 4) < 3).astype(jnp.int32), jax.random.fold_in(seeds[3], 1), 0, 1)
    adapter = plant(jax.random.randint(seeds[4], (SLOTS,), 0, ADAPTER_COUNT), jax.random.fold_in(seeds[4], 1), 0, ADAPTER_COUNT - 1).astype(jnp.int32)
    incoming_mamba_state = bell_draw(seeds[5], (SLOTS, MH, P_SIZE, NS), 1.0, 6.0, ((0, 8), (1, 4)), jnp.float32)
    mamba_norm_gain = jnp.clip(1.0 + 0.18 * jax.random.normal(seeds[6], (MODEL_WIDTH,), jnp.float32), 0.1, 1.9)
    trainer_gate_input_weight = bell_draw(seeds[7], (MODEL_WIDTH, 2, DI), MODEL_WIDTH ** -0.5, 0.09375, ((0, 32),), jnp.float32)
    trainer_step_weight = bell_draw(seeds[8], (MODEL_WIDTH, 2 * NS + MH), MODEL_WIDTH ** -0.5, 0.09375, ((0, 32),), jnp.float32)
    convolution_inner_taps = bell_draw(seeds[9], (CW, DI), 0.5, 3.0, ((1, 4),), jnp.float32)
    convolution_bc_taps = bell_draw(seeds[10], (CW, 2 * NS), 0.5, 3.0, (), jnp.float32)
    step_bias = jnp.clip(-4.0 + 3.5 * jax.random.uniform(seeds[11], (MH,), jnp.float32) ** block_levels(seeds[11], (MH,), ((0, 4),), -0.2, 0.2), -4.0, -0.5)
    head_decay_rate = jnp.clip(jnp.exp(math.log(1.0) - 2.9957323 * jax.random.uniform(seeds[12], (MH,), jnp.float32) ** block_levels(seeds[12], (MH,), ((0, 4),), -0.2, 0.2)), 0.05, 1.0)
    direct_head_term = jnp.clip(0.5 + 1.0 * jax.random.uniform(seeds[13], (MH,), jnp.float32) ** block_levels(seeds[13], (MH,), ((0, 4),), -0.2, 0.2), 0.5, 1.5)
    gated_norm_gain = jnp.clip(1.0 + 0.18 * jax.random.normal(seeds[14], (DI,), jnp.float32), 0.1, 1.9)
    trainer_mamba_output_weight = bell_draw(seeds[15], (DI, MODEL_WIDTH), DI ** -0.5, 0.09375, ((1, 32),), jnp.float32)
    attention_norm_gain = jnp.clip(1.0 + 0.18 * jax.random.normal(seeds[16], (2 * MODEL_WIDTH,), jnp.float32), 0.1, 1.9)
    trainer_query_key_value_weight = draw_trainer_query_key_value_weight(jax.random.fold_in(seeds[21], 71), 0)
    adapter_down_maps = bell_draw(seeds[18], (ADAPTER_COUNT, 2 * MODEL_WIDTH, ADAPTER_RANK), (2 * MODEL_WIDTH) ** -0.5, 0.0625)
    adapter_up_maps = bell_draw(seeds[19], (ADAPTER_COUNT, ADAPTER_RANK, 3, ATTENTION_FEATS), ADAPTER_RANK ** -0.5, 0.5, ((3, 4),))
    trainer_output_weight = bell_draw(seeds[20], (ATTENTION_FEATS, MODEL_WIDTH), ATTENTION_FEATS ** -0.5, 0.09375, ((1, 32),), jnp.float32)
    return dict(hidden=hidden, embeds=embeds, lengths=lengths, live=live, adapter=adapter, incoming_mamba_state=incoming_mamba_state, mamba_norm_gain=mamba_norm_gain, trainer_gate_input_weight=trainer_gate_input_weight, trainer_step_weight=trainer_step_weight, convolution_inner_taps=convolution_inner_taps, convolution_bc_taps=convolution_bc_taps, step_bias=step_bias, head_decay_rate=head_decay_rate, direct_head_term=direct_head_term, gated_norm_gain=gated_norm_gain, trainer_mamba_output_weight=trainer_mamba_output_weight, attention_norm_gain=attention_norm_gain, trainer_query_key_value_weight=trainer_query_key_value_weight, adapter_down_maps=adapter_down_maps, adapter_up_maps=adapter_up_maps, trainer_output_weight=trainer_output_weight)


EPSILON = 1e-05
HIGHEST = lax.Precision.HIGHEST

def normed(values, gain):
    return values * lax.rsqrt(lax.optimization_barrier(jnp.mean(values * values, axis=-1, keepdims=True)) + EPSILON) * gain

def stored(values):
    return lax.optimization_barrier(values.astype(jnp.bfloat16)).astype(jnp.float32)

def causal_conv(values, kernel):
    width = kernel.shape[0]
    seq_len = values.shape[-2]
    padding = [(0, 0)] * (values.ndim - 2) + [(width - 1, 0), (0, 0)]
    padded = jnp.pad(values, padding)
    total = jnp.zeros(values.shape, jnp.float32)
    for offset in range(width):
        total = total + kernel[offset] * padded[..., offset:offset + seq_len, :]
    return total

def rounded_sum(parts):
    return lax.optimization_barrier(jnp.sum(stored(parts), axis=0))

def attend(queries, keys, values, length):
    scale = HS ** (-0.5)
    scores = jnp.einsum('qhd,khd->hqk', queries.astype(jnp.float32), keys.astype(jnp.float32), precision=HIGHEST) * scale
    positions = jnp.arange(LEN)
    allowed = (positions[None, :] <= positions[:, None]) & (positions[None, :] < length)
    scores = jnp.where(allowed[None], scores, -1e+30)
    peak = lax.optimization_barrier(jnp.max(scores, axis=-1, keepdims=True))
    expo = jnp.exp(scores - peak)
    weights = (expo / lax.optimization_barrier(jnp.sum(expo, axis=-1, keepdims=True))).astype(jnp.bfloat16)
    mixed = jnp.einsum('hqk,khd->qhd', weights.astype(jnp.float32), values.astype(jnp.float32), precision=HIGHEST)
    return mixed.astype(jnp.bfloat16).reshape(LEN, ATTENTION_FEATS)

def ssm_scan(inputs, steps, decay, b_rows, c_rows):

    def advance(state, row):
        x_row, dt_row, decay_row, b_row, c_row = row
        state = decay_row[:, None, None] * state + (dt_row[:, None] * x_row)[:, :, None] * b_row[None, None, :]
        output = jnp.einsum('hpn,n->hp', state, c_row, precision=HIGHEST)
        return (state, output)
    start = jnp.zeros((MH, P_SIZE, NS), jnp.float32)
    final, outputs = lax.scan(advance, start, (inputs, steps, decay, b_rows, c_rows))
    return (outputs, final)

def reference(hidden, embeds, lengths, live, adapter, incoming_mamba_state, mamba_norm_gain, trainer_gate_input_weight, trainer_step_weight, convolution_inner_taps, convolution_bc_taps, step_bias, head_decay_rate, direct_head_term, gated_norm_gain, trainer_mamba_output_weight, attention_norm_gain, trainer_query_key_value_weight, adapter_down_maps, adapter_up_maps, trainer_output_weight):
    zx_server = trainer_gate_input_weight.astype(jnp.bfloat16).reshape(MODEL_WIDTH, 2 * DI)
    small_server = trainer_step_weight.astype(jnp.bfloat16)
    out_server = stored(trainer_mamba_output_weight).reshape(N_TP, DI // N_TP, MODEL_WIDTH)
    qkv_server = trainer_query_key_value_weight.astype(jnp.bfloat16).reshape(2 * MODEL_WIDTH, 3 * ATTENTION_FEATS)
    o_server = stored(trainer_output_weight).reshape(N_TP, ATTENTION_FEATS // N_TP, MODEL_WIDTH)

    def one_slot(slot):
        tokens, extra, length, active, adapter_choice, carried = slot
        stream = tokens.astype(jnp.float32)
        normed_in = normed(stream, mamba_norm_gain).astype(jnp.bfloat16)
        zx = stored(jnp.dot(normed_in, zx_server, preferred_element_type=jnp.float32))
        gate_part = zx[:, :DI]
        x_part = zx[:, DI:]
        small = stored(jnp.dot(normed_in, small_server, preferred_element_type=jnp.float32))
        x_conv = jax.nn.silu(causal_conv(x_part, convolution_inner_taps))
        bc_conv = jax.nn.silu(causal_conv(small[:, :2 * NS], convolution_bc_taps))
        valid = jnp.arange(LEN) < length
        steps = jax.nn.softplus(small[:, 2 * NS:] + step_bias) * valid[:, None].astype(jnp.float32)
        decay = jnp.exp(-steps * head_decay_rate)
        heads_in = x_conv.reshape(LEN, MH, P_SIZE)
        outputs, final = ssm_scan(heads_in, steps, decay, bc_conv[:, :NS], bc_conv[:, NS:])
        outputs = outputs + direct_head_term[:, None] * heads_in
        gated = outputs.reshape(LEN, DI) * jax.nn.silu(gate_part)
        gated = normed(gated, gated_norm_gain).astype(jnp.bfloat16)
        parts = jnp.einsum('ltk,tkd->tld', gated.astype(jnp.float32).reshape(LEN, N_TP, DI // N_TP), out_server, precision=HIGHEST)
        middle = (stream + rounded_sum(parts)).astype(jnp.bfloat16)
        joined = jnp.concatenate([middle.astype(jnp.float32), extra.astype(jnp.float32)], axis=-1)
        att_in = normed(joined, attention_norm_gain).astype(jnp.bfloat16)
        down_product = lax.dynamic_index_in_dim(adapter_down_maps, adapter_choice, 0, keepdims=False)
        chosen_up_map = lax.dynamic_index_in_dim(adapter_up_maps, adapter_choice, 0, keepdims=False).reshape(ADAPTER_RANK, 3 * ATTENTION_FEATS)
        low = jnp.dot(att_in, down_product, preferred_element_type=jnp.float32).astype(jnp.bfloat16)
        proj = jnp.dot(att_in, qkv_server, preferred_element_type=jnp.float32) + jnp.dot(low, chosen_up_map, preferred_element_type=jnp.float32)
        proj = proj.astype(jnp.bfloat16).reshape(LEN, 3, HA, HS)
        mixed = attend(proj[:, 0], proj[:, 1], proj[:, 2], length)
        parts_att = jnp.einsum('ltk,tkd->tld', mixed.astype(jnp.float32).reshape(LEN, N_TP, ATTENTION_FEATS // N_TP), o_server, precision=HIGHEST)
        result = (middle.astype(jnp.float32) + rounded_sum(parts_att)).astype(jnp.bfloat16)
        keep = (active > 0) & valid
        result = jnp.where(keep[:, None], result, jnp.zeros_like(result))
        state = jnp.where(active > 0, final, carried)
        return (result, state)
    out_hidden, out_state = lax.map(one_slot, (hidden, embeds, lengths, live, adapter, incoming_mamba_state))
    return (out_hidden, out_state)
```

```python
from functools import partial

import jax
import jax.numpy as jnp
from jax import lax
from jax.experimental import pallas as pl
from jax.experimental.pallas import tpu as pltpu
from jax.sharding import PartitionSpec as P

HS = 224
EPSILON = 1e-05
HIGHEST = lax.Precision.HIGHEST
BF = jnp.bfloat16
F32 = jnp.float32
NT = (((1,), (1,)), ((), ()))
NN = (((1,), (0,)), ((), ()))
TN = (((0,), (0,)), ((), ()))
MB = 1 << 20


def dot(a, b, dims=NN, precision=None):
    return lax.dot_general(a, b, dims, precision=precision, preferred_element_type=F32)


def params(mb):
    return pltpu.CompilerParams(vmem_limit_bytes=mb * MB)


def cost(flops, nbytes):
    return pl.CostEstimate(flops=flops, bytes_accessed=nbytes, transcendentals=0)


def exchange(value, axis, bits):
    count = lax.axis_size(axis)
    return lax.ppermute(value, axis, [(i, i ^ bits) for i in range(count)])


def after(values, waited):
    held = lax.optimization_barrier(tuple(values) + tuple(waited))
    return list(held[: len(values)])


def tp_send(slices):
    me = lax.axis_index("tp")
    return [
        exchange(lax.dynamic_index_in_dim(slices, me ^ b, 0, keepdims=False), "tp", b)
        for b in range(1, slices.shape[0])
    ]


def tp_place(slices, received):
    me = lax.axis_index("tp")
    out = slices
    for b, piece in enumerate(received, 1):
        out = lax.dynamic_update_index_in_dim(out, piece, me ^ b, 0)
    return out.reshape(-1, slices.shape[2])


class Gather:
    def __init__(self, own):
        self.own = own
        self.count = lax.axis_size("req")
        self.pieces = [(0, 0, own)]

    def first(self):
        own = self.own
        self.core = exchange(own, "req", 1)
        if self.count == 8:
            self.px, self.py = exchange(own, "req", 2), exchange(own, "req", 4)
            return [self.px, self.py]
        moved = [(0, own)]
        bit = 2
        while bit < self.count:
            moved = moved + [(at ^ bit, exchange(v, "req", bit)) for at, v in moved]
            bit *= 2
        self.moved = moved
        return [v for _, v in moved[1:]]

    def second(self):
        self.pieces.append((1, 0, self.core))
        if self.count != 8:
            self.pieces += [(at, 0, v) for at, v in self.moved[1:]]
            self.pieces += [(at ^ 1, 0, exchange(v, "req", 1)) for at, v in self.moved[1:]]
            return []
        half = -(-self.own.shape[0] // 32) * 16
        self.half = half
        self.d0 = exchange(self.py[:half], "req", 2)
        self.d1 = exchange(self.px[half:], "req", 4)
        self.pieces += [(2, 0, self.px), (4, 0, self.py)]
        self.pieces += [(3, 0, exchange(self.px, "req", 1)), (5, 0, exchange(self.py, "req", 1))]
        return [self.d0, self.d1]

    def third(self):
        if self.count != 8:
            return
        self.pieces += [(6, 0, self.d0), (6, self.half, self.d1)]
        self.pieces += [
            (7, 0, exchange(self.d0, "req", 1)),
            (7, self.half, exchange(self.d1, "req", 1)),
        ]

    def refresh(self, names, values):
        for name, value in zip(names, values):
            setattr(self, name, value)

    def whole(self):
        me = lax.axis_index("req")
        rows = self.own.shape[0]
        out = jnp.zeros((self.count * rows, self.own.shape[1]), self.own.dtype)
        for at, low, v in self.pieces:
            out = lax.dynamic_update_slice_in_dim(out, v, (me ^ at) * rows + low, 0)
        return out


def k_split_kernel(places, extra, req_ref, act_ref, *refs):
    out_ref = refs[-1]
    me = req_ref[0]
    total = None
    for (at, low, rows), w_ref in zip(places, refs):
        a = act_ref[me ^ at]
        part = dot(a[:, low : low + rows], w_ref[...])
        total = part if total is None else total + part
    if extra:
        total = total + dot(refs[-3][...], refs[-2][...])
    out_ref[...] = total.astype(BF)


def k_split_matmul(act, gathered, low=None, up=None, block=256):
    owners, tokens, depth = act.shape
    width = gathered.own.shape[1]
    me = lax.axis_index("req").astype(jnp.int32).reshape(1)
    places = [(at, first, v.shape[0]) for at, first, v in gathered.pieces]
    arrays = [v for _, _, v in gathered.pieces]
    extra = low is not None
    in_specs = [pl.BlockSpec((owners, tokens, depth), lambda n, r: (0, 0, 0))]
    in_specs += [pl.BlockSpec((v.shape[0], block), lambda n, r: (0, n)) for v in arrays]
    if extra:
        in_specs.append(pl.BlockSpec(low.shape, lambda n, r: (0, 0)))
        in_specs.append(pl.BlockSpec((up.shape[0], block), lambda n, r: (0, n)))
        arrays = arrays + [low, up]
    return pl.pallas_call(
        partial(k_split_kernel, places, extra),
        grid_spec=pltpu.PrefetchScalarGridSpec(
            num_scalar_prefetch=1,
            grid=(pl.cdiv(width, block),),
            in_specs=in_specs,
            out_specs=pl.BlockSpec((tokens, block), lambda n, r: (0, n)),
        ),
        out_shape=jax.ShapeDtypeStruct((tokens, width), BF),
        compiler_params=params(48),
        cost_estimate=cost(2 * owners * tokens * depth * width, owners * depth * width * 2),
        name="k_split",
    )(me, act, *arrays)


def scan_kernel(
    heads, inner, state_dim, chunk, info_ref, zx_ref, taps_ref, bc_taps_ref, bias_ref, bias_t_ref,
    rate_ref, rate_t_ref, direct_ref, out_ref, final_ref, pad_ref, bcpad_ref, conv_ref, bc_ref,
):
    tokens = out_ref.shape[0]
    head_dim = inner // heads
    length, first_head = info_ref[0], info_ref[1]
    width = taps_ref.shape[0]
    pad_ref[0:8, :] = jnp.zeros((8, inner), F32)
    pad_ref[8:, :] = zx_ref[:, inner : 2 * inner].astype(F32)
    bcpad_ref[0:8, :] = jnp.zeros((8, 2 * state_dim), F32)
    bcpad_ref[8:, :] = zx_ref[:, 2 * inner : 2 * inner + 2 * state_dim].astype(F32)
    for base in range(0, tokens, chunk):
        x = jnp.zeros((chunk, inner), F32)
        b = jnp.zeros((chunk, 2 * state_dim), F32)
        for k in range(width):
            low = base + 8 - (width - 1) + k
            x = x + taps_ref[k : k + 1, :] * pad_ref[low : low + chunk, :]
            b = b + bc_taps_ref[k : k + 1, :] * bcpad_ref[low : low + chunk, :]
        conv_ref[base : base + chunk, :] = x * jax.nn.sigmoid(x)
        bc_ref[base : base + chunk, :] = b * jax.nn.sigmoid(b)

    def softplus(v):
        return jnp.maximum(v, 0.0) + jnp.log1p(jnp.exp(-jnp.abs(v)))

    raw = zx_ref[:, 2 * inner + 2 * state_dim :]
    lanes = raw.shape[1]
    pick = (
        lax.broadcasted_iota(jnp.int32, (lanes, 128), 0)
        == lax.broadcasted_iota(jnp.int32, (lanes, 128), 1) + first_head
    ).astype(F32).astype(BF)
    pick_t = (
        lax.broadcasted_iota(jnp.int32, (16, lanes), 1)
        == lax.broadcasted_iota(jnp.int32, (16, lanes), 0) + first_head
    ).astype(F32).astype(BF)
    valid = lax.broadcasted_iota(jnp.int32, (tokens, 128), 0) < length
    valid_t = lax.broadcasted_iota(jnp.int32, (16, tokens), 1) < length
    steps = jnp.where(valid, softplus(dot(raw, pick) + bias_ref[...]), 0.0)
    steps_t = jnp.where(valid_t, softplus(dot(pick_t, raw, NT) + bias_t_ref[...]), 0.0)
    logs = -steps * rate_ref[...]
    logs_t = -steps_t * rate_t_ref[...]
    rows = lax.broadcasted_iota(jnp.int32, (chunk, chunk), 0)
    cols = lax.broadcasted_iota(jnp.int32, (chunk, chunk), 1)
    lower = rows >= cols
    tri = lower.astype(F32)
    tri_t = (rows <= cols).astype(F32)
    spread = (
        lax.broadcasted_iota(jnp.int32, (128, inner), 1) // head_dim
        == lax.broadcasted_iota(jnp.int32, (128, inner), 0)
    ).astype(F32)
    state = jnp.zeros((state_dim, inner), F32)
    for base in range(0, tokens, chunk):
        span = slice(base, base + chunk)
        x = conv_ref[span, :]
        bc = bc_ref[span, :]
        b_rows = bc[:, :state_dim].astype(BF)
        c_rows = bc[:, state_dim:].astype(BF)
        cumul = dot(tri, logs[span, :], precision=HIGHEST)
        cumul_t = dot(logs_t[:, span], tri_t, precision=HIGHEST)
        last = cumul[chunk - 1 : chunk, :]
        near = dot(c_rows, b_rows, NT)
        near = jnp.where(lower, near, 0.0)
        grown = dot(jnp.exp(cumul), spread, precision=HIGHEST)
        x_dt = x * dot(steps[span, :], spread, precision=HIGHEST)
        tail = dot(jnp.exp(last - cumul), spread, precision=HIGHEST)
        carried = dot(c_rows, state.astype(BF)) * grown
        x_dt_b = x_dt.astype(BF)
        direct = direct_ref[...] * x + carried
        gate = zx_ref[span, :inner].astype(F32)
        gate = gate * jax.nn.sigmoid(gate)
        per = 128 // head_dim
        for tile in range(pl.cdiv(heads, per)):
            left, right = tile * 128, min(tile * 128 + 128, inner)
            lane = lax.broadcasted_iota(jnp.int32, (chunk, right - left), 1)
            within = jnp.zeros((chunk, right - left), F32)
            for h in range(tile * per, min(tile * per + per, heads)):
                gap = cumul[:, h : h + 1] - cumul_t[h : h + 1, :]
                gap = jnp.where(lower, gap, -1e30)
                weights = (near * jnp.exp(gap)).astype(BF)
                part = dot(weights, x_dt_b[:, left:right])
                mine = lane // head_dim == h - tile * per
                within = jnp.where(mine, part, within)
            y = (within + direct[:, left:right]) * gate[:, left:right]
            out_ref[span, left:right] = y.astype(BF)
        fresh = dot(b_rows, (x_dt * tail).astype(BF), TN)
        kept = dot(jnp.broadcast_to(jnp.exp(last), (8, 128)), spread, precision=HIGHEST)[0:1, :]
        state = state * kept + fresh
    final_ref[...] = state.T


def run_scan(zx, info, taps, bc_taps, bias, rate, direct, heads, inner, state_dim):
    tokens = zx.shape[0]

    def padded(v):
        return (
            jnp.pad(v[None, :], ((0, 0), (0, 128 - heads))),
            jnp.pad(v[:, None], ((0, 16 - heads), (0, 0))),
        )

    bias_r, bias_c = padded(bias)
    rate_r, rate_c = padded(rate)
    spread = jnp.repeat(direct, inner // heads)[None, :]
    vm = pl.BlockSpec(memory_space=pltpu.VMEM)
    return pl.pallas_call(
        partial(scan_kernel, heads, inner, state_dim, 128),
        in_specs=[pl.BlockSpec(memory_space=pltpu.SMEM)] + [vm] * 8,
        out_specs=(vm, vm),
        out_shape=(
            jax.ShapeDtypeStruct((tokens, inner), BF),
            jax.ShapeDtypeStruct((inner, state_dim), F32),
        ),
        scratch_shapes=[
            pltpu.VMEM((tokens + 8, inner), F32),
            pltpu.VMEM((tokens + 8, 2 * state_dim), F32),
            pltpu.VMEM((tokens, inner), F32),
            pltpu.VMEM((tokens, 2 * state_dim), F32),
        ],
        compiler_params=params(40),
        cost_estimate=cost(6 * 10**9, 4 * MB),
        name="scan",
    )(info, zx, taps, bc_taps, bias_r, bias_c, rate_r, rate_c, spread)


def mixer_kernel(places, tp_count, ordered, idx_ref, *refs):
    g_refs, gain_ref, stream_ref = refs[:tp_count], refs[tp_count], refs[tp_count + 1]
    w_refs, out_ref = refs[tp_count + 2 : -1], refs[-1]
    req, tp = idx_ref[0], 0 if ordered else idx_ref[1]
    tokens, share = g_refs[0].shape
    acts = []
    squares = jnp.zeros((8, tokens), F32)
    ones = jnp.ones((8, share), F32)
    for b in range(tp_count):
        raw = g_refs[b][...].astype(F32)
        squares = squares + dot(ones, raw * raw, NT, precision=HIGHEST)
        acts.append((raw * gain_ref[tp ^ b]).astype(BF))
    scale = lax.rsqrt(squares[0:1, :] / (share * tp_count) + EPSILON)
    for (at, low, rows), w_ref in zip(places, w_refs):
        total = None
        for b in range(tp_count):
            if ordered:
                weights = w_ref[:, b * share : (b + 1) * share]
            else:
                weights = w_ref[:, pl.ds(pl.multiple_of((tp ^ b) * share, 128), share)]
            part = dot(weights, acts[b], NT)
            total = part if total is None else total + part
        if at is None:
            to = 0
        else:
            to = pl.multiple_of((req ^ at) * (out_ref.shape[0] // 8) + low, 16)
        span = pl.ds(to, rows)
        out_ref[span, :] = (stream_ref[span, :].astype(F32) + total * scale).astype(BF)


def mixer(gathered, idx, raws, gain, stream):
    rows = gathered.own.shape[0]
    if rows % 16 or gathered.count != 8:
        weights, places = [gathered.whole()], [(None, 0, gathered.count * rows)]
    else:
        weights = [v for _, _, v in gathered.pieces]
        places = [(at, low, v.shape[0]) for at, low, v in gathered.pieces]
    ordered = raws[0].shape[1] % 128 != 0
    if ordered:
        stacked = jnp.stack(raws)
        for b, raw in enumerate(raws):
            stacked = lax.dynamic_update_index_in_dim(stacked, raw, idx[1] ^ b, 0)
        raws = [stacked[i] for i in range(len(raws))]
    vm = pl.BlockSpec(memory_space=pltpu.VMEM)
    return pl.pallas_call(
        partial(mixer_kernel, places, len(raws), ordered),
        in_specs=[pl.BlockSpec(memory_space=pltpu.SMEM)] + [vm] * (len(raws) + 2 + len(weights)),
        out_specs=vm,
        out_shape=jax.ShapeDtypeStruct(stream.shape, BF),
        compiler_params=params(48),
        cost_estimate=cost(2 * 896 * 384 * 3584, 12 * MB),
        name="mixer",
    )(idx, *raws, gain, stream, *weights)


def join_kernel(which_ref, mid_ref, embeds_ref, gain_ref, down_ref, act_ref, low_ref):
    owners, tokens, depth = act_ref.shape
    half = owners // 2
    squares = jnp.zeros((tokens, 1), F32)
    for i in range(owners):
        if i < half:
            part = mid_ref[i * depth : (i + 1) * depth, :].astype(F32).T
        else:
            part = embeds_ref[:, (i - half) * depth : (i - half + 1) * depth].astype(F32)
        squares = squares + jnp.sum(part * part, axis=1, keepdims=True)
        act_ref[i] = part.astype(BF)
    scale = lax.rsqrt(squares / (owners * depth) + EPSILON)
    low = jnp.zeros((tokens, down_ref.shape[2]), F32)
    for i in range(owners):
        gain = gain_ref[:, i * depth : (i + 1) * depth]
        value = (act_ref[i].astype(F32) * scale * gain).astype(BF)
        act_ref[i] = value
        low = low + dot(value, down_ref[0, i * depth : (i + 1) * depth, :])
    low_ref[...] = low.astype(BF)


def join(mid, embeds, gain, down, which, owners):
    width, tokens = mid.shape
    depth = 2 * width // owners
    rank = down.shape[2]
    return pl.pallas_call(
        join_kernel,
        grid_spec=pltpu.PrefetchScalarGridSpec(
            num_scalar_prefetch=1,
            grid=(1,),
            in_specs=[
                pl.BlockSpec((width, tokens), lambda i, a: (0, 0)),
                pl.BlockSpec((tokens, width), lambda i, a: (0, 0)),
                pl.BlockSpec((1, 2 * width), lambda i, a: (0, 0)),
                pl.BlockSpec((1, 2 * width, rank), lambda i, a: (a[0], 0, 0)),
            ],
            out_specs=(
                pl.BlockSpec((owners, tokens, depth), lambda i, a: (0, 0, 0)),
                pl.BlockSpec((tokens, rank), lambda i, a: (0, 0)),
            ),
        ),
        out_shape=(
            jax.ShapeDtypeStruct((owners, tokens, depth), BF),
            jax.ShapeDtypeStruct((tokens, rank), BF),
        ),
        compiler_params=params(48),
        cost_estimate=cost(2 * 7168 * 384 * 128, 13 * MB),
        name="join",
    )(which, mid, embeds, gain, down)


def attend_kernel(heads, size, info_ref, q_ref, k_ref, v_ref, out_ref):
    tokens, width = q_ref.shape
    length = info_ref[0]
    rows = lax.broadcasted_iota(jnp.int32, (tokens, tokens), 0)
    cols = lax.broadcasted_iota(jnp.int32, (tokens, tokens), 1)
    allowed = (cols <= rows) & (cols < length)
    spans = []
    for h in range(heads):
        left = h * size // 128 * 128
        right = min(-(-(h + 1) * size // 128) * 128, width)
        spans.append((left, right))
    done = {}
    for h, (left, right) in enumerate(spans):
        lane = lax.broadcasted_iota(jnp.int32, (tokens, right - left), 1) + left
        mine = (lane >= h * size) & (lane < (h + 1) * size)
        query = jnp.where(mine, q_ref[:, left:right].astype(F32), 0.0).astype(BF)
        scores = dot(query, k_ref[:, left:right], NT) * size ** (-0.5)
        scores = jnp.where(allowed, scores, -1e30)
        peak = jnp.max(scores, axis=1, keepdims=True)
        expo = jnp.exp(scores - peak)
        weights = (expo / jnp.sum(expo, axis=1, keepdims=True)).astype(BF)
        mixed = dot(weights, v_ref[:, left:right])
        mixed = jnp.where(mine, mixed, 0.0)
        for at in range(left, right, 128):
            to = min(at + 128, right)
            part = mixed[:, at - left : to - left]
            done[at] = part if at not in done else done[at] + part
    for at, value in done.items():
        out_ref[:, at : at + value.shape[1]] = value.astype(BF)


def attend(q, k, v, info, heads):
    vm = pl.BlockSpec(memory_space=pltpu.VMEM)
    return pl.pallas_call(
        partial(attend_kernel, heads, HS),
        in_specs=[pl.BlockSpec(memory_space=pltpu.SMEM), vm, vm, vm],
        out_specs=vm,
        out_shape=jax.ShapeDtypeStruct(q.shape, BF),
        compiler_params=params(40),
        cost_estimate=cost(6 * 10**9, 3 * MB),
        name="attend",
    )(info, q, k, v)


def output_kernel(places, idx_ref, act_ref, *refs):
    out_ref = refs[-1]
    me = idx_ref[0]
    each = refs[0].shape[0]
    for (at, low, rows), w_ref in zip(places, refs):
        to = pl.multiple_of((me ^ at) * each + low, 16)
        out_ref[pl.ds(to, rows), :] = dot(w_ref[...], act_ref[...], NT).astype(BF)


def output_product(gathered, idx, act):
    weights = [v for _, _, v in gathered.pieces]
    places = [(at, low, v.shape[0]) for at, low, v in gathered.pieces]
    vm = pl.BlockSpec(memory_space=pltpu.VMEM)
    return pl.pallas_call(
        partial(output_kernel, places),
        in_specs=[pl.BlockSpec(memory_space=pltpu.SMEM)] + [vm] * (1 + len(weights)),
        out_specs=vm,
        out_shape=jax.ShapeDtypeStruct((gathered.count * gathered.own.shape[0], act.shape[0]), BF),
        compiler_params=params(40),
        cost_estimate=cost(2 * 896 * 384 * 3584, 10 * MB),
        name="output",
    )(idx, act, *weights)


def finish_kernel(info_ref, mid_ref, *refs):
    out_ref = refs[-1]
    total = mid_ref[...].astype(F32)
    for ref in refs[:-1]:
        total = total + ref[...].astype(F32)
    total = total.T
    rows = lax.broadcasted_iota(jnp.int32, total.shape, 0)
    keep = rows < jnp.where(info_ref[1] > 0, info_ref[0], 0)
    out_ref[...] = jnp.where(keep, total, 0.0).astype(BF)


def finish(info, mid, parts):
    vm = pl.BlockSpec(memory_space=pltpu.VMEM)
    return pl.pallas_call(
        finish_kernel,
        in_specs=[pl.BlockSpec(memory_space=pltpu.SMEM)] + [vm] * (1 + len(parts)),
        out_specs=vm,
        out_shape=jax.ShapeDtypeStruct((mid.shape[1], mid.shape[0]), BF),
        compiler_params=params(24),
        cost_estimate=cost(10**6, 4 * MB),
        name="finish",
    )(info, mid, *parts)


def local(
    hidden,
    embeds,
    lengths,
    live,
    adapter,
    incoming_mamba_state,
    mamba_norm_gain,
    trainer_gate_input_weight,
    trainer_step_weight,
    convolution_inner_taps,
    convolution_bc_taps,
    step_bias,
    head_decay_rate,
    direct_head_term,
    gated_norm_gain,
    trainer_mamba_output_weight,
    attention_norm_gain,
    trainer_query_key_value_weight,
    adapter_down_maps,
    adapter_up_maps,
    trainer_output_weight,
):
    tp_count, req_count = lax.axis_size("tp"), lax.axis_size("req")
    tp_index = lax.axis_index("tp").astype(jnp.int32)
    req_index = lax.axis_index("req").astype(jnp.int32)
    idx = jnp.stack([req_index, tp_index])
    _, seq_len, width = hidden.shape
    heads = step_bias.shape[0]
    inner = convolution_inner_taps.shape[1]
    state_dim = convolution_bc_taps.shape[1] // 2
    rows = trainer_gate_input_weight.shape[0]

    out_t = trainer_mamba_output_weight.astype(BF).T
    small = trainer_step_weight.astype(BF)
    small = jnp.pad(small, ((0, 0), (0, 256 - small.shape[1])))
    gate_input = trainer_gate_input_weight.astype(BF)
    zx_slices = jnp.concatenate(
        [
            gate_input[:, 0].reshape(rows, tp_count, inner),
            gate_input[:, 1].reshape(rows, tp_count, inner),
            jnp.broadcast_to(small[:, None, :], (rows, tp_count, 256)),
        ],
        axis=2,
    ).transpose(1, 0, 2)

    def qkv_slices(i):
        piece = trainer_query_key_value_weight[:, i].astype(BF)
        return piece.reshape(piece.shape[0], tp_count, -1).transpose(1, 0, 2)

    gain_all = lax.all_gather(gated_norm_gain, "tp", axis=0, tiled=False)[:, None, :]

    mamba_out = Gather(out_t)
    zx_received = tp_send(zx_slices)
    out_first = mamba_out.first()
    zx_own = tp_place(zx_slices, zx_received)

    stream = hidden[0].astype(F32)
    normed_in = stream * lax.rsqrt(jnp.mean(stream * stream, axis=-1, keepdims=True) + EPSILON)
    normed_in = (normed_in * mamba_norm_gain).astype(BF)
    normed_in = normed_in.reshape(seq_len, req_count, -1).transpose(1, 0, 2)
    stream_t = hidden[0].T.reshape(req_count, tp_count, rows, seq_len)
    stream_t = lax.dynamic_index_in_dim(stream_t, tp_index, 1, keepdims=False)
    stream_t = stream_t.reshape(req_count * rows, seq_len)

    q_slices = qkv_slices(0)
    held = after([zx_own, q_slices] + out_first, [mamba_out.core])
    zx_own, q_slices = held[:2]
    if req_count == 8:
        mamba_out.refresh(["px", "py"], held[2:])
    zx_gather = Gather(zx_own)
    zx_first = zx_gather.first()
    out_second = mamba_out.second()
    q_received = tp_send(q_slices)
    q_own = tp_place(q_slices, q_received)

    k_slices = qkv_slices(1)
    held = after([k_slices, q_own] + zx_first + out_second, [zx_gather.core])
    k_slices, q_own = held[:2]
    if req_count == 8:
        zx_gather.refresh(["px", "py"], held[2:4])
        mamba_out.refresh(["d0", "d1"], held[4:])
    zx_second = zx_gather.second()
    mamba_out.third()
    k_received = tp_send(k_slices)
    k_own = tp_place(k_slices, k_received)

    v_slices = qkv_slices(2)
    held = after([v_slices, k_own, q_own] + zx_second, [])
    v_slices, k_own, q_own = held[:3]
    if req_count == 8:
        zx_gather.refresh(["d0", "d1"], held[3:])
    q_gather = Gather(q_own)
    q_first = q_gather.first()
    zx_gather.third()
    v_received = tp_send(v_slices)
    v_own = tp_place(v_slices, v_received)

    zx = k_split_matmul(normed_in, zx_gather)
    info = jnp.stack([lengths[0], tp_index * heads])
    raw, final = run_scan(
        zx, info, convolution_inner_taps, convolution_bc_taps, step_bias, head_decay_rate,
        direct_head_term, heads, inner, state_dim,
    )

    o_t = trainer_output_weight.astype(BF).T
    o_slices = o_t.reshape(rows, tp_count, -1).transpose(1, 0, 2)
    held = after([o_slices, v_own, k_own] + q_first, [q_gather.core])
    o_slices, v_own, k_own = held[:3]
    if req_count == 8:
        q_gather.refresh(["px", "py"], held[3:])
    q_second = q_gather.second()
    k_gather = Gather(k_own)
    k_first = k_gather.first()
    raws = [raw] + [exchange(raw, "tp", b) for b in range(1, tp_count)]
    o_own = tp_place(o_slices, tp_send(o_slices))

    held = after([v_own, o_own] + k_first + q_second, [k_gather.core])
    v_own, o_own = held[:2]
    if req_count == 8:
        k_gather.refresh(["px", "py"], held[2:4])
        q_gather.refresh(["d0", "d1"], held[4:])
    k_second = k_gather.second()
    q_gather.third()
    v_gather = Gather(v_own)
    v_first = v_gather.first()

    mid_own = mixer(mamba_out, idx, raws, gain_all, stream_t)
    mids = jnp.zeros((tp_count,) + mid_own.shape, BF)
    for b in range(tp_count):
        moved = exchange(mid_own, "tp", b) if b else mid_own
        mids = lax.dynamic_update_index_in_dim(mids, moved, tp_index ^ b, 0)
    mid = mids.reshape(tp_count, req_count, rows, seq_len).transpose(1, 0, 2, 3)
    mid = mid.reshape(width, seq_len)

    held = after([o_own] + v_first + k_second, [v_gather.core])
    o_own = held[0]
    if req_count == 8:
        v_gather.refresh(["px", "py"], held[1:3])
        k_gather.refresh(["d0", "d1"], held[3:])
    v_second = v_gather.second()
    k_gather.third()
    o_gather = Gather(o_own)
    o_first = o_gather.first()

    act, low = join(
        mid, embeds[0], attention_norm_gain[None, :], adapter_down_maps, adapter, req_count
    )
    ups = lax.dynamic_index_in_dim(adapter_up_maps, adapter[0], 0, keepdims=False)
    ups = [ups[:, i] for i in range(3)]
    queries = k_split_matmul(act, q_gather, low, ups[0])
    keys = k_split_matmul(act, k_gather, low, ups[1])

    held = after(o_first + v_second, [o_gather.core])
    if req_count == 8:
        o_gather.refresh(["px", "py"], held[:2])
        v_gather.refresh(["d0", "d1"], held[2:])
    v_gather.third()
    o_second = o_gather.second()
    o_gather.third()

    values = k_split_matmul(act, v_gather, low, ups[2])
    attended = attend(queries, keys, values, lengths, queries.shape[1] // HS)
    share = output_product(o_gather, idx, attended).reshape(tp_count, -1, seq_len)
    parts = [lax.dynamic_index_in_dim(share, tp_index, 0, keepdims=False)]
    parts += tp_send(share)
    mid_share = lax.dynamic_slice_in_dim(mid, tp_index * parts[0].shape[0], parts[0].shape[0], 0)
    result = finish(jnp.stack([lengths[0], live[0]]), mid_share, parts)
    final = final.reshape((1, heads, inner // heads, state_dim))
    state = jnp.where((live > 0)[:, None, None, None], final, incoming_mamba_state)
    return (result[None], state)


def solution(mesh):
    placed = (
        P("req", None, None),
        P("req", None, None),
        P("req"),
        P("req"),
        P("req"),
        P("req", "tp", None, None),
        P(),
        P(("req", "tp"), None, None),
        P(("req", "tp"), None),
        P(None, "tp"),
        P(),
        P("tp"),
        P("tp"),
        P("tp"),
        P("tp"),
        P(None, ("req", "tp")),
        P(),
        P(("req", "tp"), None, None),
        P(),
        P(None, None, None, "tp"),
        P(None, ("req", "tp")),
    )
    return jax.shard_map(
        local,
        mesh=mesh,
        in_specs=placed,
        out_specs=(P("req", None, "tp"), P("req", "tp", None, None)),
        check_vma=False,
    )
```

```python
from functools import partial

import jax
import jax.numpy as jnp
from jax import lax
from jax.experimental import pallas as pl
from jax.experimental.pallas import tpu as pltpu
from jax.sharding import PartitionSpec as P

HS = 224
EPSILON = 1e-05
HIGHEST = lax.Precision.HIGHEST
BF = jnp.bfloat16
F32 = jnp.float32
NT = (((1,), (1,)), ((), ()))
NN = (((1,), (0,)), ((), ()))
TN = (((0,), (0,)), ((), ()))
MB = 1 << 20


def dot(a, b, dims=NN, precision=None):
    return lax.dot_general(a, b, dims, precision=precision, preferred_element_type=F32)


def params(mb):
    return pltpu.CompilerParams(vmem_limit_bytes=mb * MB)


def cost(flops, nbytes):
    return pl.CostEstimate(flops=flops, bytes_accessed=nbytes, transcendentals=0)


def exchange(value, axis, bits):
    count = lax.axis_size(axis)
    return lax.ppermute(value, axis, [(i, i ^ bits) for i in range(count)])


def after(values, waited):
    held = lax.optimization_barrier(tuple(values) + tuple(waited))
    return list(held[: len(values)])


def prepare_input_kernel(idx_ref, w_ref, small_ref, *outs):
    tp = idx_ref[1]
    count = len(outs)
    share = w_ref.shape[2] // count
    for k in range(2):
        for t in range(count):
            piece = w_ref[k, :, t * share : (t + 1) * share].astype(BF)
            for b in range(count):

                @pl.when(tp ^ b == t)
                def _():
                    outs[b][:, k * share : (k + 1) * share] = piece

    for b in range(count):
        outs[b][:, 2 * share :] = small_ref[...]


def prepare_input(idx, weight, small, count):
    _, rows, width = weight.shape
    cols = 2 * width // count + small.shape[1]
    vm = pl.BlockSpec(memory_space=pltpu.VMEM)
    outs = pl.pallas_call(
        prepare_input_kernel,
        in_specs=[pl.BlockSpec(memory_space=pltpu.SMEM), vm, vm],
        out_specs=(vm,) * count,
        out_shape=(jax.ShapeDtypeStruct((rows, cols), BF),) * count,
        compiler_params=params(32),
        cost_estimate=cost(10**6, 6 * MB),
        name="prepare_input",
    )(idx, weight, small)
    return list(outs)


def prepare_kernel(groups, w_ref, *outs):
    for out_ref, parts in zip(outs, groups):
        count = out_ref.shape[0]
        share = w_ref.shape[2] // count
        for j, k in enumerate(parts):
            for t in range(count):
                piece = w_ref[k, :, t * share : (t + 1) * share].astype(BF)
                out_ref[t, :, j * share : (j + 1) * share] = piece


def prepare(weight, count, groups):
    parts, rows, width = weight.shape
    share = width // count
    block = rows // 2 if rows % 32 == 0 else rows
    shapes = [jax.ShapeDtypeStruct((count, rows, share * len(g)), BF) for g in groups]
    return pl.pallas_call(
        partial(prepare_kernel, groups),
        grid=(rows // block,),
        in_specs=[pl.BlockSpec((parts, block, width), lambda i: (0, i, 0))],
        out_specs=tuple(pl.BlockSpec((count, block, v.shape[2]), lambda i: (0, i, 0)) for v in shapes),
        out_shape=tuple(shapes),
        compiler_params=params(40),
        cost_estimate=cost(10**6, parts * rows * width * 6),
        name="prepare",
    )(weight)


def tp_trade(slices):
    out = lax.all_to_all(slices, "tp", split_axis=0, concat_axis=0, tiled=True)
    return out.reshape(-1, slices.shape[2])


def norm_kernel(x_ref, gain_ref, out_ref):
    depth = out_ref.shape[2]
    x = x_ref[...].astype(F32)
    scale = lax.rsqrt(jnp.mean(x * x, axis=1, keepdims=True) + EPSILON)
    for i in range(out_ref.shape[0]):
        span = slice(i * depth, (i + 1) * depth)
        out_ref[i] = (x_ref[:, span].astype(F32) * scale * gain_ref[:, span]).astype(BF)


def norm(x, gain, owners):
    tokens, width = x.shape
    vm = pl.BlockSpec(memory_space=pltpu.VMEM)
    return pl.pallas_call(
        norm_kernel,
        in_specs=[vm, vm],
        out_specs=vm,
        out_shape=jax.ShapeDtypeStruct((owners, tokens, width // owners), BF),
        compiler_params=params(32),
        cost_estimate=cost(10**7, 6 * MB),
        name="norm",
    )(x, gain)


def tp_send(pieces):
    return [pieces[0]] + [exchange(p, "tp", b) for b, p in enumerate(pieces) if b]


def by_xor(slices):
    me = lax.axis_index("tp")
    return [
        lax.dynamic_index_in_dim(slices, me ^ b, 0, keepdims=False) for b in range(slices.shape[0])
    ]


def place_kernel(idx_ref, *refs):
    out_ref = refs[-1]
    rows = refs[0].shape[0]
    for b, ref in enumerate(refs[:-1]):
        out_ref[pl.ds(pl.multiple_of((idx_ref[1] ^ b) * rows, 16), rows), :] = ref[...]


def tp_place(idx, received):
    count = len(received)
    rows, cols = received[0].shape
    if rows % 16:
        out = jnp.zeros((count, rows, cols), BF)
        for b, piece in enumerate(received):
            out = lax.dynamic_update_index_in_dim(out, piece, idx[1] ^ b, 0)
        return out.reshape(count * rows, cols)
    vm = pl.BlockSpec(memory_space=pltpu.VMEM)
    return pl.pallas_call(
        place_kernel,
        in_specs=[pl.BlockSpec(memory_space=pltpu.SMEM)] + [vm] * count,
        out_specs=vm,
        out_shape=jax.ShapeDtypeStruct((count * rows, cols), BF),
        compiler_params=params(24),
        cost_estimate=cost(10**6, 2 * count * rows * cols * 2),
        name="place",
    )(idx, *received)


def gather_rows(piece):
    return lax.all_gather(piece, "req", axis=0, tiled=True)


class Gather:
    def __init__(self, own):
        self.own = own
        self.count = lax.axis_size("req")
        self.pieces = [(0, 0, own)]

    def first(self):
        own = self.own
        if self.count == 8:
            self.px, self.py = exchange(own, "req", 2), exchange(own, "req", 4)
            return [self.px, self.py]
        moved = [(0, own)]
        bit = 2
        while bit < self.count:
            moved = moved + [(at ^ bit, exchange(v, "req", bit)) for at, v in moved]
            bit *= 2
        self.moved = moved
        return [v for _, v in moved[1:]]

    def second(self):
        if self.count != 8:
            self.pieces = [(at, 0, v) for at, v in self.moved]
            self.pieces += [(at ^ 1, 0, exchange(v, "req", 1)) for at, v in self.moved]
            return []
        half = -(-self.own.shape[0] // 32) * 16
        self.half = half
        self.d0 = exchange(self.py[:half], "req", 2)
        self.d1 = exchange(self.px[half:], "req", 4)
        self.pieces.append((1, 0, exchange(self.own, "req", 1)))
        self.pieces += [(2, 0, self.px), (4, 0, self.py)]
        self.pieces += [(3, 0, exchange(self.px, "req", 1)), (5, 0, exchange(self.py, "req", 1))]
        return [self.d0, self.d1]

    def third(self):
        if self.count != 8:
            return
        self.pieces += [(6, 0, self.d0), (6, self.half, self.d1)]
        self.pieces += [
            (7, 0, exchange(self.d0, "req", 1)),
            (7, self.half, exchange(self.d1, "req", 1)),
        ]

    def refresh(self, names, values):
        for name, value in zip(names, values):
            setattr(self, name, value)


def pieces_kernel(places, req_ref, act_ref, *refs):
    count = len(places)
    out_ref, buf_ref, acc_ref, sems = refs[count:]
    me = req_ref[0]
    width = acc_ref.shape[1]
    starts = []
    total = 0
    for _, _, rows in places:
        starts.append(total)
        total += rows

    def copy(i):
        rows = places[i][2]
        return pltpu.make_async_copy(
            refs[i], buf_ref.at[starts[i] : starts[i] + rows, :], sems.at[i]
        )

    for i in range(count):
        copy(i).start()
    for i, (at, low, rows) in enumerate(places):
        copy(i).wait()
        a = act_ref[me ^ at][:, low : low + rows]
        for left in range(0, width, 512):
            span = slice(left, min(left + 512, width))
            part = dot(a, buf_ref[starts[i] : starts[i] + rows, span])
            if i:
                part = part + acc_ref[:, span]
            if i < count - 1:
                acc_ref[:, span] = part
            else:
                out_ref[:, span] = part.astype(BF)


def pieces_matmul(act, gathered):
    owners, tokens, depth = act.shape
    width = gathered.own.shape[1]
    me = lax.axis_index("req").astype(jnp.int32).reshape(1)
    places = [(at, first, v.shape[0]) for at, first, v in gathered.pieces]
    arrays = [v for _, _, v in gathered.pieces]
    vm = pl.BlockSpec(memory_space=pltpu.VMEM)
    return pl.pallas_call(
        partial(pieces_kernel, places),
        in_specs=[pl.BlockSpec(memory_space=pltpu.SMEM), vm]
        + [pl.BlockSpec(memory_space=pl.ANY)] * len(arrays),
        out_specs=vm,
        out_shape=jax.ShapeDtypeStruct((tokens, width), BF),
        scratch_shapes=[
            pltpu.VMEM((owners * depth, width), BF),
            pltpu.VMEM((tokens, width), F32),
            pltpu.SemaphoreType.DMA((len(arrays),)),
        ],
        compiler_params=params(40),
        cost_estimate=cost(2 * owners * tokens * depth * width, owners * depth * width * 2),
        name="zx",
    )(me, act, *arrays)


def rows_kernel(act_ref, w_ref, low_ref, up_ref, out_ref, acc_ref):
    step = pl.program_id(0)
    part = dot(act_ref[0], w_ref[...])

    @pl.when(step == 0)
    def _():
        acc_ref[...] = part + dot(low_ref[...], up_ref[...])

    @pl.when((step > 0) & (step < pl.num_programs(0) - 1))
    def _():
        acc_ref[...] += part

    @pl.when(step == pl.num_programs(0) - 1)
    def _():
        out_ref[...] = (acc_ref[...] + part).astype(BF)


def rows_matmul(act, weight, low, up):
    owners, tokens, depth = act.shape
    width = weight.shape[1]
    return pl.pallas_call(
        rows_kernel,
        grid=(owners,),
        in_specs=[
            pl.BlockSpec((1, tokens, depth), lambda i: (i, 0, 0)),
            pl.BlockSpec((depth, width), lambda i: (i, 0)),
            pl.BlockSpec(low.shape, lambda i: (0, 0)),
            pl.BlockSpec(up.shape, lambda i: (0, 0)),
        ],
        out_specs=pl.BlockSpec((tokens, width), lambda i: (0, 0)),
        out_shape=jax.ShapeDtypeStruct((tokens, width), BF),
        scratch_shapes=[pltpu.VMEM((tokens, width), F32)],
        compiler_params=params(58),
        cost_estimate=cost(2 * owners * tokens * depth * width, owners * depth * width * 2),
        name="qkv",
    )(act, weight, low, up)


def scan_kernel(
    heads, inner, state_dim, chunk, info_ref, zx_ref, taps_ref, bc_taps_ref, bias_ref, bias_t_ref,
    rate_ref, rate_t_ref, direct_ref, out_ref, final_ref, pad_ref, bcpad_ref, conv_ref, bc_ref,
):
    tokens = out_ref.shape[0]
    head_dim = inner // heads
    length, first_head = info_ref[0], info_ref[1]
    width = taps_ref.shape[0]
    pad_ref[0:8, :] = jnp.zeros((8, inner), F32)
    pad_ref[8:, :] = zx_ref[:, inner : 2 * inner].astype(F32)
    bcpad_ref[0:8, :] = jnp.zeros((8, 2 * state_dim), F32)
    bcpad_ref[8:, :] = zx_ref[:, 2 * inner : 2 * inner + 2 * state_dim].astype(F32)
    for base in range(0, tokens, chunk):
        x = jnp.zeros((chunk, inner), F32)
        b = jnp.zeros((chunk, 2 * state_dim), F32)
        for k in range(width):
            low = base + 8 - (width - 1) + k
            x = x + taps_ref[k : k + 1, :] * pad_ref[low : low + chunk, :]
            b = b + bc_taps_ref[k : k + 1, :] * bcpad_ref[low : low + chunk, :]
        conv_ref[base : base + chunk, :] = x * jax.nn.sigmoid(x)
        bc_ref[base : base + chunk, :] = b * jax.nn.sigmoid(b)

    def softplus(v):
        return jnp.maximum(v, 0.0) + jnp.log1p(jnp.exp(-jnp.abs(v)))

    raw = zx_ref[:, 2 * inner + 2 * state_dim :]
    lanes = raw.shape[1]
    pick = (
        lax.broadcasted_iota(jnp.int32, (lanes, 128), 0)
        == lax.broadcasted_iota(jnp.int32, (lanes, 128), 1) + first_head
    ).astype(F32).astype(BF)
    pick_t = (
        lax.broadcasted_iota(jnp.int32, (16, lanes), 1)
        == lax.broadcasted_iota(jnp.int32, (16, lanes), 0) + first_head
    ).astype(F32).astype(BF)
    valid = lax.broadcasted_iota(jnp.int32, (tokens, 128), 0) < length
    valid_t = lax.broadcasted_iota(jnp.int32, (16, tokens), 1) < length
    steps = jnp.where(valid, softplus(dot(raw, pick) + bias_ref[...]), 0.0)
    steps_t = jnp.where(valid_t, softplus(dot(pick_t, raw, NT) + bias_t_ref[...]), 0.0)
    logs = -steps * rate_ref[...]
    logs_t = -steps_t * rate_t_ref[...]
    rows = lax.broadcasted_iota(jnp.int32, (chunk, chunk), 0)
    cols = lax.broadcasted_iota(jnp.int32, (chunk, chunk), 1)
    lower = rows >= cols
    tri = lower.astype(F32)
    tri_t = (rows <= cols).astype(F32)
    spread = (
        lax.broadcasted_iota(jnp.int32, (128, inner), 1) // head_dim
        == lax.broadcasted_iota(jnp.int32, (128, inner), 0)
    ).astype(F32)
    state = jnp.zeros((state_dim, inner), F32)
    for base in range(0, tokens, chunk):
        span = slice(base, base + chunk)
        x = conv_ref[span, :]
        bc = bc_ref[span, :]
        b_rows = bc[:, :state_dim].astype(BF)
        c_rows = bc[:, state_dim:].astype(BF)
        cumul = dot(tri, logs[span, :], precision=HIGHEST)
        cumul_t = dot(logs_t[:, span], tri_t, precision=HIGHEST)
        last = cumul[chunk - 1 : chunk, :]
        near = dot(c_rows, b_rows, NT)
        near = jnp.where(lower, near, 0.0)
        grown = dot(jnp.exp(cumul), spread, precision=HIGHEST)
        x_dt = x * dot(steps[span, :], spread, precision=HIGHEST)
        tail = dot(jnp.exp(last - cumul), spread, precision=HIGHEST)
        carried = dot(c_rows, state.astype(BF)) * grown
        x_dt_b = x_dt.astype(BF)
        direct = direct_ref[...] * x + carried
        gate = zx_ref[span, :inner].astype(F32)
        gate = gate * jax.nn.sigmoid(gate)
        per = 128 // head_dim
        for tile in range(pl.cdiv(heads, per)):
            left, right = tile * 128, min(tile * 128 + 128, inner)
            lane = lax.broadcasted_iota(jnp.int32, (chunk, right - left), 1)
            within = jnp.zeros((chunk, right - left), F32)
            for h in range(tile * per, min(tile * per + per, heads)):
                gap = cumul[:, h : h + 1] - cumul_t[h : h + 1, :]
                gap = jnp.where(lower, gap, -1e30)
                weights = (near * jnp.exp(gap)).astype(BF)
                part = dot(weights, x_dt_b[:, left:right])
                mine = lane // head_dim == h - tile * per
                within = jnp.where(mine, part, within)
            y = (within + direct[:, left:right]) * gate[:, left:right]
            out_ref[span, left:right] = y.astype(BF)
        fresh = dot(b_rows, (x_dt * tail).astype(BF), TN)
        kept = dot(jnp.broadcast_to(jnp.exp(last), (8, 128)), spread, precision=HIGHEST)[0:1, :]
        state = state * kept + fresh
    final_ref[...] = state.T


def head_rows(bias, rate, direct, heads, inner):
    def padded(v):
        return [
            jnp.pad(v[None, :], ((0, 0), (0, 128 - heads))),
            jnp.pad(v[:, None], ((0, 16 - heads), (0, 0))),
        ]

    return padded(bias) + padded(rate) + [jnp.repeat(direct, inner // heads)[None, :]]


def run_scan(zx, info, taps, bc_taps, per_head, heads, inner, state_dim):
    tokens = zx.shape[0]
    vm = pl.BlockSpec(memory_space=pltpu.VMEM)
    return pl.pallas_call(
        partial(scan_kernel, heads, inner, state_dim, 128),
        in_specs=[pl.BlockSpec(memory_space=pltpu.SMEM)] + [vm] * 8,
        out_specs=(vm, vm),
        out_shape=(
            jax.ShapeDtypeStruct((tokens, inner), BF),
            jax.ShapeDtypeStruct((inner, state_dim), F32),
        ),
        scratch_shapes=[
            pltpu.VMEM((tokens + 8, inner), F32),
            pltpu.VMEM((tokens + 8, 2 * state_dim), F32),
            pltpu.VMEM((tokens, inner), F32),
            pltpu.VMEM((tokens, 2 * state_dim), F32),
        ],
        compiler_params=params(40),
        cost_estimate=cost(6 * 10**9, 4 * MB),
        name="scan",
    )(info, zx, taps, bc_taps, *per_head)


def column_weights(gathered, which):
    owners, _, rows, width = gathered.shape
    if rows % 16:
        gathered = gathered[:, which].reshape(1, 1, owners * rows, width)
        which = 0
    block = (gathered.shape[0], 1) + gathered.shape[2:]
    return gathered, pl.BlockSpec(block, lambda i, x: (0, which, 0, 0))


def columns_kernel(tp_count, ordered, scaled, idx_ref, *refs):
    a_refs, gain_ref, stream_ref, w_ref, out_ref = refs[:tp_count], *refs[tp_count:]
    tp = 0 if ordered else idx_ref[1]
    tokens, share = a_refs[0].shape
    rows = out_ref.shape[0]
    squares = jnp.zeros((tokens, 1), F32)
    total = None
    for b in range(tp_count):
        act = a_refs[b][...]
        if scaled:
            raw = act.astype(F32)
            squares = squares + jnp.sum(raw * raw, axis=1, keepdims=True)
            act = (raw * gain_ref[tp ^ b]).astype(BF)
        if ordered:
            weights = w_ref[:, 0, :, b * share : (b + 1) * share]
        else:
            weights = w_ref[:, 0, :, pl.ds(pl.multiple_of((tp ^ b) * share, 128), share)]
        part = dot(weights.reshape(rows, share), act, NT)
        total = part if total is None else total + part
    if scaled:
        scale = lax.rsqrt(squares / (share * tp_count) + EPSILON)
        total = total * jnp.broadcast_to(scale, (tokens, 128)).T[0:1, :]
        out_ref[...] = (stream_ref[...].astype(F32) + total).astype(BF)
    else:
        total = stream_ref[...].astype(F32) + total
        place = lax.broadcasted_iota(jnp.int32, total.shape, 1)
        keep = place < jnp.where(idx_ref[3] > 0, idx_ref[2], 0)
        out_ref[...] = jnp.where(keep, total, 0.0).astype(BF)


def columns(gathered, which, idx, parts, gain, stream, scaled):
    ordered = parts[0].shape[1] % 128 != 0
    if ordered:
        stacked = jnp.stack(parts)
        for b, part in enumerate(parts):
            stacked = lax.dynamic_update_index_in_dim(stacked, part, idx[1] ^ b, 0)
        parts = [stacked[i] for i in range(len(parts))]
    weights, spec = column_weights(gathered, which)

    def full(v):
        return pl.BlockSpec(v.shape, lambda i, x: (0,) * v.ndim)

    return pl.pallas_call(
        partial(columns_kernel, len(parts), ordered, scaled),
        grid_spec=pltpu.PrefetchScalarGridSpec(
            num_scalar_prefetch=1,
            grid=(1,),
            in_specs=[full(v) for v in parts] + [full(gain), full(stream), spec],
            out_specs=full(stream),
        ),
        out_shape=jax.ShapeDtypeStruct(stream.shape, BF),
        compiler_params=params(58),
        cost_estimate=cost(2 * 896 * 384 * 3584, 12 * MB),
        name="mixer" if scaled else "output",
    )(idx, *parts, gain, stream, weights)


def join_kernel(which_ref, mid_ref, embeds_ref, gain_ref, down_ref, act_ref, low_ref):
    owners, tokens, depth = act_ref.shape
    half = owners // 2
    squares = jnp.zeros((tokens, 1), F32)
    for i in range(owners):
        if i < half:
            part = mid_ref[i * depth : (i + 1) * depth, :].astype(F32).T
        else:
            part = embeds_ref[:, (i - half) * depth : (i - half + 1) * depth].astype(F32)
        squares = squares + jnp.sum(part * part, axis=1, keepdims=True)
        act_ref[i] = part.astype(BF)
    scale = lax.rsqrt(squares / (owners * depth) + EPSILON)
    low = jnp.zeros((tokens, down_ref.shape[2]), F32)
    for i in range(owners):
        gain = gain_ref[:, i * depth : (i + 1) * depth]
        value = (act_ref[i].astype(F32) * scale * gain).astype(BF)
        act_ref[i] = value
        low = low + dot(value, down_ref[0, i * depth : (i + 1) * depth, :])
    low_ref[...] = low.astype(BF)


def join(mid, embeds, gain, down, which, owners):
    width, tokens = mid.shape
    depth = 2 * width // owners
    rank = down.shape[2]
    return pl.pallas_call(
        join_kernel,
        grid_spec=pltpu.PrefetchScalarGridSpec(
            num_scalar_prefetch=1,
            grid=(1,),
            in_specs=[
                pl.BlockSpec((width, tokens), lambda i, a: (0, 0)),
                pl.BlockSpec((tokens, width), lambda i, a: (0, 0)),
                pl.BlockSpec((1, 2 * width), lambda i, a: (0, 0)),
                pl.BlockSpec((1, 2 * width, rank), lambda i, a: (a[0], 0, 0)),
            ],
            out_specs=(
                pl.BlockSpec((owners, tokens, depth), lambda i, a: (0, 0, 0)),
                pl.BlockSpec((tokens, rank), lambda i, a: (0, 0)),
            ),
        ),
        out_shape=(
            jax.ShapeDtypeStruct((owners, tokens, depth), BF),
            jax.ShapeDtypeStruct((tokens, rank), BF),
        ),
        compiler_params=params(48),
        cost_estimate=cost(2 * 7168 * 384 * 128, 13 * MB),
        name="join",
    )(which, mid, embeds, gain, down)


def attend_kernel(heads, size, info_ref, q_ref, kv_ref, out_ref):
    tokens, width = q_ref.shape
    length = info_ref[0]
    rows = lax.broadcasted_iota(jnp.int32, (tokens, tokens), 0)
    cols = lax.broadcasted_iota(jnp.int32, (tokens, tokens), 1)
    allowed = (cols <= rows) & (cols < length)
    spans = []
    for h in range(heads):
        left = h * size // 128 * 128
        right = min(-(-(h + 1) * size // 128) * 128, width)
        spans.append((left, right))
    done = {}
    for h, (left, right) in enumerate(spans):
        lane = lax.broadcasted_iota(jnp.int32, (tokens, right - left), 1) + left
        mine = (lane >= h * size) & (lane < (h + 1) * size)
        query = jnp.where(mine, q_ref[:, left:right].astype(F32), 0.0).astype(BF)
        scores = dot(query, kv_ref[:, left:right], NT) * size ** (-0.5)
        scores = jnp.where(allowed, scores, -1e30)
        peak = jnp.max(scores, axis=1, keepdims=True)
        expo = jnp.exp(scores - peak)
        weights = (expo / jnp.sum(expo, axis=1, keepdims=True)).astype(BF)
        mixed = dot(weights, kv_ref[:, width + left : width + right])
        mixed = jnp.where(mine, mixed, 0.0)
        for at in range(left, right, 128):
            to = min(at + 128, right)
            part = mixed[:, at - left : to - left]
            done[at] = part if at not in done else done[at] + part
    for at, value in done.items():
        out_ref[:, at : at + value.shape[1]] = value.astype(BF)


def attend(q, kv, info, heads):
    vm = pl.BlockSpec(memory_space=pltpu.VMEM)
    return pl.pallas_call(
        partial(attend_kernel, heads, HS),
        in_specs=[pl.BlockSpec(memory_space=pltpu.SMEM), vm, vm],
        out_specs=vm,
        out_shape=jax.ShapeDtypeStruct(q.shape, BF),
        compiler_params=params(40),
        cost_estimate=cost(6 * 10**9, 3 * MB),
        name="attend",
    )(info, q, kv)


def finish_kernel(rows, idx_ref, *refs):
    out_ref, all_ref = refs[-2:]
    count = len(refs) - 2
    groups = refs[0].shape[0] // rows
    for g in range(groups):
        for b, ref in enumerate(refs[:-2]):
            to = pl.multiple_of((g * count + (idx_ref[1] ^ b)) * rows, 16)
            all_ref[pl.ds(to, rows), :] = ref[g * rows : (g + 1) * rows, :]
    out_ref[...] = all_ref[...].astype(F32).T.astype(BF)


def finish(idx, parts, rows):
    count = len(parts)
    tokens = parts[0].shape[1]
    if rows % 16:
        out = jnp.zeros((parts[0].shape[0] // rows, count, rows, tokens), BF)
        for b, part in enumerate(parts):
            part = part.reshape(-1, 1, rows, tokens)
            out = lax.dynamic_update_slice_in_dim(out, part, idx[1] ^ b, 1)
        return out.reshape(-1, tokens).T
    vm = pl.BlockSpec(memory_space=pltpu.VMEM)
    width = count * parts[0].shape[0]
    return pl.pallas_call(
        partial(finish_kernel, rows),
        in_specs=[pl.BlockSpec(memory_space=pltpu.SMEM)] + [vm] * count,
        out_specs=vm,
        out_shape=jax.ShapeDtypeStruct((tokens, width), BF),
        scratch_shapes=[pltpu.VMEM((width, tokens), BF)],
        compiler_params=params(24),
        cost_estimate=cost(10**6, 2 * MB),
        name="finish",
    )(idx, *parts)


def local(
    hidden,
    embeds,
    lengths,
    live,
    adapter,
    incoming_mamba_state,
    mamba_norm_gain,
    trainer_gate_input_weight,
    trainer_step_weight,
    convolution_inner_taps,
    convolution_bc_taps,
    step_bias,
    head_decay_rate,
    direct_head_term,
    gated_norm_gain,
    trainer_mamba_output_weight,
    attention_norm_gain,
    trainer_query_key_value_weight,
    adapter_down_maps,
    adapter_up_maps,
    trainer_output_weight,
):
    tp_count, req_count = lax.axis_size("tp"), lax.axis_size("req")
    tp_index = lax.axis_index("tp").astype(jnp.int32)
    req_index = lax.axis_index("req").astype(jnp.int32)
    idx = jnp.stack([req_index, tp_index, lengths[0], live[0]])
    _, seq_len, width = hidden.shape
    heads = step_bias.shape[0]
    inner = convolution_inner_taps.shape[1]
    state_dim = convolution_bc_taps.shape[1] // 2
    rows = trainer_gate_input_weight.shape[0]

    small = trainer_step_weight.astype(BF)
    high = lax.optimization_barrier(gated_norm_gain.astype(BF))
    rest = (gated_norm_gain - high.astype(F32)).astype(BF)
    small = jnp.concatenate([small, high.reshape(rows, -1), rest.reshape(rows, -1)], axis=1)
    used, each = trainer_step_weight.shape[1], inner // rows
    small = jnp.pad(small, ((0, 0), (0, 256 - small.shape[1])))
    zx_send = prepare_input(idx, trainer_gate_input_weight.transpose(1, 0, 2), small, tp_count)
    zx_received = tp_send(zx_send)
    o_pair = jnp.stack([trainer_mamba_output_weight.astype(BF).T, trainer_output_weight.astype(BF).T])
    o_pair = gather_rows(o_pair[None])
    q_send, kv_send = prepare(
        trainer_query_key_value_weight.transpose(1, 0, 2), tp_count, [(0,), (1, 2)]
    )
    normed_in = norm(hidden[0], mamba_norm_gain[None, :], req_count)
    per_head = head_rows(step_bias, head_decay_rate, direct_head_term, heads, inner)
    zx_own = tp_place(idx, zx_received)

    zx_own, q_send, *_ = after([zx_own, q_send], [normed_in] + per_head)
    zx_gather = Gather(zx_own)
    zx_first = zx_gather.first()
    q_own = tp_trade(q_send)
    stream_t = hidden[0].T.reshape(req_count, tp_count, rows, seq_len)
    stream_t = lax.dynamic_index_in_dim(stream_t, tp_index, 1, keepdims=False)
    stream_t = stream_t.reshape(req_count * rows, seq_len)
    ups = lax.dynamic_index_in_dim(adapter_up_maps, adapter[0], 0, keepdims=False)
    ups = [ups[:, 0], ups[:, 1:].reshape(ups.shape[0], -1)]
    gain_all = zx_own.reshape(tp_count, rows, -1)[:, :, 2 * inner + used :].astype(F32)
    gain_all = (gain_all[:, :, :each] + gain_all[:, :, each : 2 * each]).reshape(tp_count, 1, inner)

    held = after(zx_first + [kv_send, q_own], [stream_t, gain_all] + ups)
    if req_count == 8:
        zx_gather.refresh(["px", "py"], held[:2])
    kv_send, q_own = held[-2:]
    q_server = gather_rows(q_own)
    zx_second = zx_gather.second()
    kv_own = tp_trade(kv_send)
    zx_gather.third()

    zx = pieces_matmul(normed_in, zx_gather)
    info = jnp.stack([lengths[0], tp_index * heads])
    raw, final = run_scan(
        zx, info, convolution_inner_taps, convolution_bc_taps, per_head, heads, inner, state_dim
    )
    raw, kv_own = after([raw, kv_own], [])
    kv_server = gather_rows(kv_own)
    raws = tp_send([raw] * tp_count)
    mid_own = columns(o_pair, 0, idx, raws, gain_all, stream_t, True)
    mids = jnp.zeros((tp_count,) + mid_own.shape, BF)
    for b, moved in enumerate(tp_send([mid_own] * tp_count)):
        mids = lax.dynamic_update_index_in_dim(mids, moved, tp_index ^ b, 0)
    mid = mids.reshape(tp_count, req_count, rows, seq_len).transpose(1, 0, 2, 3)
    mid = mid.reshape(width, seq_len)
    act, low = join(mid, embeds[0], attention_norm_gain[None, :], adapter_down_maps, adapter, 4)
    queries = rows_matmul(act, q_server, low, ups[0])
    keys_values = rows_matmul(act, kv_server, low, ups[1])
    attended = attend(queries, keys_values, lengths, queries.shape[1] // HS)
    whole = tp_send([attended] * tp_count)
    result = columns(o_pair, 1, idx, whole, gain_all, mid_own, False)
    result = tp_send(by_xor(result.reshape(tp_count, -1, seq_len)))
    result = finish(idx, result, rows)
    final = final.reshape((1, heads, inner // heads, state_dim))
    state = jnp.where((live > 0)[:, None, None, None], final, incoming_mamba_state)
    return (result[None], state)


def solution(mesh):
    placed = (
        P("req", None, None),
        P("req", None, None),
        P("req"),
        P("req"),
        P("req"),
        P("req", "tp", None, None),
        P(),
        P(("req", "tp"), None, None),
        P(("req", "tp"), None),
        P(None, "tp"),
        P(),
        P("tp"),
        P("tp"),
        P("tp"),
        P("tp"),
        P(None, ("req", "tp")),
        P(),
        P(("req", "tp"), None, None),
        P(),
        P(None, None, None, "tp"),
        P(None, ("req", "tp")),
    )
    return jax.shard_map(
        local,
        mesh=mesh,
        in_specs=placed,
        out_specs=(P("req", None, "tp"), P("req", "tp", None, None)),
        check_vma=False,
    )
```

```python
from functools import partial

import jax
import jax.numpy as jnp
from jax import lax
from jax.experimental import pallas as pl
from jax.experimental.pallas import tpu as pltpu
from jax.sharding import PartitionSpec as P

HS = 224
EPSILON = 1e-05
HIGHEST = lax.Precision.HIGHEST
BF = jnp.bfloat16
F32 = jnp.float32
NT = (((1,), (1,)), ((), ()))
NN = (((1,), (0,)), ((), ()))
TN = (((0,), (0,)), ((), ()))
MB = 1 << 20


def dot(a, b, dims=NN, precision=None):
    return lax.dot_general(a, b, dims, precision=precision, preferred_element_type=F32)


def params(mb):
    return pltpu.CompilerParams(vmem_limit_bytes=mb * MB)


def cost(flops, nbytes):
    return pl.CostEstimate(flops=flops, bytes_accessed=nbytes, transcendentals=0)


def exchange(value, axis, bits):
    count = lax.axis_size(axis)
    return lax.ppermute(value, axis, [(i, i ^ bits) for i in range(count)])


def after(values, waited):
    held = lax.optimization_barrier(tuple(values) + tuple(waited))
    return list(held[: len(values)])


def prepare_input_kernel(idx_ref, w_ref, small_ref, *outs):
    tp = idx_ref[1]
    count = len(outs)
    share = w_ref.shape[2] // count
    for k in range(2):
        for t in range(count):
            piece = w_ref[k, :, t * share : (t + 1) * share].astype(BF)
            for b in range(count):

                @pl.when(tp ^ b == t)
                def _():
                    outs[b][:, k * share : (k + 1) * share] = piece

    for b in range(count):
        outs[b][:, 2 * share :] = small_ref[...]


def prepare_input(idx, weight, small, count):
    _, rows, width = weight.shape
    cols = 2 * width // count + small.shape[1]
    vm = pl.BlockSpec(memory_space=pltpu.VMEM)
    outs = pl.pallas_call(
        prepare_input_kernel,
        in_specs=[pl.BlockSpec(memory_space=pltpu.SMEM), vm, vm],
        out_specs=(vm,) * count,
        out_shape=(jax.ShapeDtypeStruct((rows, cols), BF),) * count,
        compiler_params=params(32),
        cost_estimate=cost(10**6, 6 * MB),
        name="prepare_input",
    )(idx, weight, small)
    return list(outs)


def prepare_kernel(groups, w_ref, *outs):
    for out_ref, parts in zip(outs, groups):
        count = out_ref.shape[0]
        share = w_ref.shape[2] // count
        for j, k in enumerate(parts):
            for t in range(count):
                piece = w_ref[k, :, t * share : (t + 1) * share].astype(BF)
                out_ref[t, :, j * share : (j + 1) * share] = piece


def prepare(weight, count, groups):
    parts, rows, width = weight.shape
    share = width // count
    block = rows // 2 if rows % 32 == 0 else rows
    shapes = [jax.ShapeDtypeStruct((count, rows, share * len(g)), BF) for g in groups]
    return pl.pallas_call(
        partial(prepare_kernel, groups),
        grid=(rows // block,),
        in_specs=[pl.BlockSpec((parts, block, width), lambda i: (0, i, 0))],
        out_specs=tuple(pl.BlockSpec((count, block, v.shape[2]), lambda i: (0, i, 0)) for v in shapes),
        out_shape=tuple(shapes),
        compiler_params=params(40),
        cost_estimate=cost(10**6, parts * rows * width * 6),
        name="prepare",
    )(weight)


def tp_trade(slices):
    out = lax.all_to_all(slices, "tp", split_axis=0, concat_axis=0, tiled=True)
    return out.reshape(-1, slices.shape[2])


def norm_kernel(x_ref, gain_ref, out_ref):
    depth = out_ref.shape[2]
    x = x_ref[...].astype(F32)
    scale = lax.rsqrt(jnp.mean(x * x, axis=1, keepdims=True) + EPSILON)
    for i in range(out_ref.shape[0]):
        span = slice(i * depth, (i + 1) * depth)
        out_ref[i] = (x_ref[:, span].astype(F32) * scale * gain_ref[:, span]).astype(BF)


def norm(x, gain, owners):
    tokens, width = x.shape
    vm = pl.BlockSpec(memory_space=pltpu.VMEM)
    return pl.pallas_call(
        norm_kernel,
        in_specs=[vm, vm],
        out_specs=vm,
        out_shape=jax.ShapeDtypeStruct((owners, tokens, width // owners), BF),
        compiler_params=params(32),
        cost_estimate=cost(10**7, 6 * MB),
        name="norm",
    )(x, gain)


def tp_send(pieces):
    return [pieces[0]] + [exchange(p, "tp", b) for b, p in enumerate(pieces) if b]


def tp_step(pair):
    count = lax.axis_size("tp")
    return (
        lax.ppermute(pair[0], "tp", [(i, i + 1) for i in range(count - 1)]),
        lax.ppermute(pair[1], "tp", [(i + 1, i) for i in range(count - 1)]),
    )


def tp_line(own):
    pairs = [(own, own)]
    for _ in range(lax.axis_size("tp") - 1):
        pairs.append(tp_step(pairs[-1]))
    return pairs


def tp_stack(pairs, tp_index):
    count = len(pairs)
    out = jnp.zeros((count,) + pairs[0][0].shape, pairs[0][0].dtype)
    out = lax.dynamic_update_index_in_dim(out, pairs[0][0], tp_index, 0)
    for j in range(1, count):
        piece = jnp.where(tp_index >= j, pairs[j][0], pairs[count - j][1])
        out = lax.dynamic_update_index_in_dim(out, piece, (tp_index - j) % count, 0)
    return out


def by_xor(slices):
    me = lax.axis_index("tp")
    return [
        lax.dynamic_index_in_dim(slices, me ^ b, 0, keepdims=False) for b in range(slices.shape[0])
    ]


def place_kernel(idx_ref, *refs):
    out_ref = refs[-1]
    rows = refs[0].shape[0]
    for b, ref in enumerate(refs[:-1]):
        out_ref[pl.ds(pl.multiple_of((idx_ref[1] ^ b) * rows, 16), rows), :] = ref[...]


def tp_place(idx, received):
    count = len(received)
    rows, cols = received[0].shape
    if rows % 16:
        out = jnp.zeros((count, rows, cols), BF)
        for b, piece in enumerate(received):
            out = lax.dynamic_update_index_in_dim(out, piece, idx[1] ^ b, 0)
        return out.reshape(count * rows, cols)
    vm = pl.BlockSpec(memory_space=pltpu.VMEM)
    return pl.pallas_call(
        place_kernel,
        in_specs=[pl.BlockSpec(memory_space=pltpu.SMEM)] + [vm] * count,
        out_specs=vm,
        out_shape=jax.ShapeDtypeStruct((count * rows, cols), BF),
        compiler_params=params(24),
        cost_estimate=cost(10**6, 2 * count * rows * cols * 2),
        name="place",
    )(idx, *received)


def gather_rows(piece):
    return lax.all_gather(piece, "req", axis=0, tiled=True)


class Gather:
    def __init__(self, own):
        self.own = own
        self.count = lax.axis_size("req")
        self.pieces = [(0, 0, own)]

    def first(self):
        own = self.own
        self.core = exchange(own, "req", 1)
        if self.count == 8:
            self.px, self.py = exchange(own, "req", 2), exchange(own, "req", 4)
            return [self.px, self.py]
        moved = [(0, own)]
        bit = 2
        while bit < self.count:
            moved = moved + [(at ^ bit, exchange(v, "req", bit)) for at, v in moved]
            bit *= 2
        self.moved = moved
        return [v for _, v in moved[1:]]

    def second(self):
        if self.count != 8:
            self.pieces = [(at, 0, v) for at, v in self.moved]
            self.pieces += [(at ^ 1, 0, exchange(v, "req", 1)) for at, v in self.moved[1:]]
            self.pieces.append((1, 0, self.core))
            return []
        half = -(-self.own.shape[0] // 32) * 16
        self.half = half
        self.d0 = exchange(self.py[:half], "req", 2)
        self.d1 = exchange(self.px[half:], "req", 4)
        self.pieces.append((1, 0, self.core))
        self.pieces += [(2, 0, self.px), (4, 0, self.py)]
        self.pieces += [(3, 0, exchange(self.px, "req", 1)), (5, 0, exchange(self.py, "req", 1))]
        return [self.d0, self.d1]

    def third(self):
        if self.count != 8:
            return
        self.pieces += [(6, 0, self.d0), (6, self.half, self.d1)]
        self.pieces += [
            (7, 0, exchange(self.d0, "req", 1)),
            (7, self.half, exchange(self.d1, "req", 1)),
        ]

    def refresh(self, names, values):
        for name, value in zip(names, values):
            setattr(self, name, value)


def pieces_kernel(places, req_ref, act_ref, *refs):
    count = len(places)
    out_ref, buf_ref, acc_ref, sems = refs[count:]
    me = req_ref[0]
    width = acc_ref.shape[1]
    starts = []
    total = 0
    for _, _, rows in places:
        starts.append(total)
        total += rows

    def copy(i):
        rows = places[i][2]
        return pltpu.make_async_copy(
            refs[i], buf_ref.at[starts[i] : starts[i] + rows, :], sems.at[i]
        )

    for i in range(count):
        copy(i).start()
    for i, (at, low, rows) in enumerate(places):
        copy(i).wait()
        a = act_ref[me ^ at][:, low : low + rows]
        for left in range(0, width, 512):
            span = slice(left, min(left + 512, width))
            part = dot(a, buf_ref[starts[i] : starts[i] + rows, span])
            if i:
                part = part + acc_ref[:, span]
            if i < count - 1:
                acc_ref[:, span] = part
            else:
                out_ref[:, span] = part.astype(BF)


def pieces_matmul(act, gathered):
    owners, tokens, depth = act.shape
    width = gathered.own.shape[1]
    me = lax.axis_index("req").astype(jnp.int32).reshape(1)
    places = [(at, first, v.shape[0]) for at, first, v in gathered.pieces]
    arrays = [v for _, _, v in gathered.pieces]
    vm = pl.BlockSpec(memory_space=pltpu.VMEM)
    return pl.pallas_call(
        partial(pieces_kernel, places),
        in_specs=[pl.BlockSpec(memory_space=pltpu.SMEM), vm]
        + [pl.BlockSpec(memory_space=pl.ANY)] * len(arrays),
        out_specs=vm,
        out_shape=jax.ShapeDtypeStruct((tokens, width), BF),
        scratch_shapes=[
            pltpu.VMEM((owners * depth, width), BF),
            pltpu.VMEM((tokens, width), F32),
            pltpu.SemaphoreType.DMA((len(arrays),)),
        ],
        compiler_params=params(40),
        cost_estimate=cost(2 * owners * tokens * depth * width, owners * depth * width * 2),
        name="zx",
    )(me, act, *arrays)


def rows_kernel(act_ref, w_ref, low_ref, up_ref, out_ref, acc_ref):
    step = pl.program_id(0)
    part = dot(act_ref[0], w_ref[...])

    @pl.when(step == 0)
    def _():
        acc_ref[...] = part + dot(low_ref[...], up_ref[...])

    @pl.when((step > 0) & (step < pl.num_programs(0) - 1))
    def _():
        acc_ref[...] += part

    @pl.when(step == pl.num_programs(0) - 1)
    def _():
        out_ref[...] = (acc_ref[...] + part).astype(BF)


def rows_matmul(act, weight, low, up):
    owners, tokens, depth = act.shape
    width = weight.shape[1]
    return pl.pallas_call(
        rows_kernel,
        grid=(owners,),
        in_specs=[
            pl.BlockSpec((1, tokens, depth), lambda i: (i, 0, 0)),
            pl.BlockSpec((depth, width), lambda i: (i, 0)),
            pl.BlockSpec(low.shape, lambda i: (0, 0)),
            pl.BlockSpec(up.shape, lambda i: (0, 0)),
        ],
        out_specs=pl.BlockSpec((tokens, width), lambda i: (0, 0)),
        out_shape=jax.ShapeDtypeStruct((tokens, width), BF),
        scratch_shapes=[pltpu.VMEM((tokens, width), F32)],
        compiler_params=params(58),
        cost_estimate=cost(2 * owners * tokens * depth * width, owners * depth * width * 2),
        name="qkv",
    )(act, weight, low, up)


def scan_kernel(
    heads, inner, state_dim, chunk, info_ref, zx_ref, taps_ref, bc_taps_ref, bias_ref, bias_t_ref,
    rate_ref, rate_t_ref, direct_ref, out_ref, final_ref, pad_ref, bcpad_ref, conv_ref, bc_ref,
):
    tokens = out_ref.shape[0]
    head_dim = inner // heads
    length, first_head = info_ref[0], info_ref[1]
    width = taps_ref.shape[0]
    pad_ref[0:8, :] = jnp.zeros((8, inner), F32)
    pad_ref[8:, :] = zx_ref[:, inner : 2 * inner].astype(F32)
    bcpad_ref[0:8, :] = jnp.zeros((8, 2 * state_dim), F32)
    bcpad_ref[8:, :] = zx_ref[:, 2 * inner : 2 * inner + 2 * state_dim].astype(F32)
    for base in range(0, tokens, chunk):
        x = jnp.zeros((chunk, inner), F32)
        b = jnp.zeros((chunk, 2 * state_dim), F32)
        for k in range(width):
            low = base + 8 - (width - 1) + k
            x = x + taps_ref[k : k + 1, :] * pad_ref[low : low + chunk, :]
            b = b + bc_taps_ref[k : k + 1, :] * bcpad_ref[low : low + chunk, :]
        conv_ref[base : base + chunk, :] = x * jax.nn.sigmoid(x)
        bc_ref[base : base + chunk, :] = b * jax.nn.sigmoid(b)

    def softplus(v):
        return jnp.maximum(v, 0.0) + jnp.log1p(jnp.exp(-jnp.abs(v)))

    raw = zx_ref[:, 2 * inner + 2 * state_dim :]
    lanes = raw.shape[1]
    pick = (
        lax.broadcasted_iota(jnp.int32, (lanes, 128), 0)
        == lax.broadcasted_iota(jnp.int32, (lanes, 128), 1) + first_head
    ).astype(F32).astype(BF)
    pick_t = (
        lax.broadcasted_iota(jnp.int32, (16, lanes), 1)
        == lax.broadcasted_iota(jnp.int32, (16, lanes), 0) + first_head
    ).astype(F32).astype(BF)
    valid = lax.broadcasted_iota(jnp.int32, (tokens, 128), 0) < length
    valid_t = lax.broadcasted_iota(jnp.int32, (16, tokens), 1) < length
    steps = jnp.where(valid, softplus(dot(raw, pick) + bias_ref[...]), 0.0)
    steps_t = jnp.where(valid_t, softplus(dot(pick_t, raw, NT) + bias_t_ref[...]), 0.0)
    logs = -steps * rate_ref[...]
    logs_t = -steps_t * rate_t_ref[...]
    rows = lax.broadcasted_iota(jnp.int32, (chunk, chunk), 0)
    cols = lax.broadcasted_iota(jnp.int32, (chunk, chunk), 1)
    lower = rows >= cols
    tri = lower.astype(F32)
    tri_t = (rows <= cols).astype(F32)
    spread = (
        lax.broadcasted_iota(jnp.int32, (128, inner), 1) // head_dim
        == lax.broadcasted_iota(jnp.int32, (128, inner), 0)
    ).astype(F32)
    state = jnp.zeros((state_dim, inner), F32)
    for base in range(0, tokens, chunk):
        span = slice(base, base + chunk)
        x = conv_ref[span, :]
        bc = bc_ref[span, :]
        b_rows = bc[:, :state_dim].astype(BF)
        c_rows = bc[:, state_dim:].astype(BF)
        cumul = dot(tri, logs[span, :], precision=HIGHEST)
        cumul_t = dot(logs_t[:, span], tri_t, precision=HIGHEST)
        last = cumul[chunk - 1 : chunk, :]
        near = dot(c_rows, b_rows, NT)
        near = jnp.where(lower, near, 0.0)
        grown = dot(jnp.exp(cumul), spread, precision=HIGHEST)
        x_dt = x * dot(steps[span, :], spread, precision=HIGHEST)
        tail = dot(jnp.exp(last - cumul), spread, precision=HIGHEST)
        carried = dot(c_rows, state.astype(BF)) * grown
        x_dt_b = x_dt.astype(BF)
        direct = direct_ref[...] * x + carried
        gate = zx_ref[span, :inner].astype(F32)
        gate = gate * jax.nn.sigmoid(gate)
        per = 128 // head_dim
        for tile in range(pl.cdiv(heads, per)):
            left, right = tile * 128, min(tile * 128 + 128, inner)
            lane = lax.broadcasted_iota(jnp.int32, (chunk, right - left), 1)
            within = jnp.zeros((chunk, right - left), F32)
            for h in range(tile * per, min(tile * per + per, heads)):
                gap = cumul[:, h : h + 1] - cumul_t[h : h + 1, :]
                gap = jnp.where(lower, gap, -1e30)
                weights = (near * jnp.exp(gap)).astype(BF)
                part = dot(weights, x_dt_b[:, left:right])
                mine = lane // head_dim == h - tile * per
                within = jnp.where(mine, part, within)
            y = (within + direct[:, left:right]) * gate[:, left:right]
            out_ref[span, left:right] = y.astype(BF)
        fresh = dot(b_rows, (x_dt * tail).astype(BF), TN)
        kept = dot(jnp.broadcast_to(jnp.exp(last), (8, 128)), spread, precision=HIGHEST)[0:1, :]
        state = state * kept + fresh
    final_ref[...] = state.T


def head_rows(bias, rate, direct, heads, inner):
    def padded(v):
        return [
            jnp.pad(v[None, :], ((0, 0), (0, 128 - heads))),
            jnp.pad(v[:, None], ((0, 16 - heads), (0, 0))),
        ]

    return padded(bias) + padded(rate) + [jnp.repeat(direct, inner // heads)[None, :]]


def run_scan(zx, info, taps, bc_taps, per_head, heads, inner, state_dim):
    tokens = zx.shape[0]
    vm = pl.BlockSpec(memory_space=pltpu.VMEM)
    return pl.pallas_call(
        partial(scan_kernel, heads, inner, state_dim, 128),
        in_specs=[pl.BlockSpec(memory_space=pltpu.SMEM)] + [vm] * 8,
        out_specs=(vm, vm),
        out_shape=(
            jax.ShapeDtypeStruct((tokens, inner), BF),
            jax.ShapeDtypeStruct((inner, state_dim), F32),
        ),
        scratch_shapes=[
            pltpu.VMEM((tokens + 8, inner), F32),
            pltpu.VMEM((tokens + 8, 2 * state_dim), F32),
            pltpu.VMEM((tokens, inner), F32),
            pltpu.VMEM((tokens, 2 * state_dim), F32),
        ],
        compiler_params=params(40),
        cost_estimate=cost(6 * 10**9, 4 * MB),
        name="scan",
    )(info, zx, taps, bc_taps, *per_head)


def columns_part(scaled, steps, idx_ref, refs):
    each = 3 if scaled else 2
    squares = total = None
    for i, step in enumerate(steps):
        act_ref, w_ref = refs[each * i], refs[each * i + 1]
        act = act_ref[...]
        if scaled:
            raw = act.astype(F32)
            square = jnp.sum(raw * raw, axis=1, keepdims=True)
            squares = square if squares is None else squares + square
            act = (raw * refs[each * i + 2][0]).astype(BF)
        part = dot(w_ref[...], act, NT)
        total = part if total is None else total + part
    return total, squares


def columns_kernel(scaled, steps, begin, last, denominator, idx_ref, *refs):
    count = (3 if scaled else 2) * len(steps)
    total, squares = columns_part(scaled, steps, idx_ref, refs)
    rest = list(refs[count:])
    if not begin:
        total = total + rest.pop(0)[...]
        if scaled:
            squares = squares + rest.pop(0)[...]
    if not last:
        rest[0][...] = total
        if scaled:
            rest[1][...] = jnp.broadcast_to(squares, rest[1].shape)
        return
    stream_ref, out_ref = rest
    if scaled:
        scale = lax.rsqrt(squares / denominator + EPSILON)
        total = total * scale.T[0:1, :]
    total = stream_ref[...].astype(F32) + total
    if not scaled:
        place = lax.broadcasted_iota(jnp.int32, total.shape, 1)
        keep = place < jnp.where(idx_ref[3] > 0, idx_ref[2], 0)
        total = jnp.where(keep, total, 0.0)
    out_ref[...] = total.astype(BF)


def columns_whole(weights, idx, pairs, gain, stream, scaled):
    acts = tp_stack(pairs, idx[1])
    count, tokens, share = acts.shape
    raw = acts.astype(F32)
    if scaled:
        acts = (raw * gain).astype(BF)
    flat = acts.transpose(1, 0, 2).reshape(tokens, count * share)
    total = dot(weights, flat, NT)
    if scaled:
        squares = jnp.sum(raw * raw, axis=(0, 2)) / (count * share)
        total = total * lax.rsqrt(squares + EPSILON)[None, :]
    total = stream.astype(F32) + total
    if not scaled:
        total = jnp.where(jnp.arange(tokens)[None, :] < idx[2] * (idx[3] > 0), total, 0.0)
    return total.astype(BF)


def columns(weights, idx, own, beside, gain, stream, scaled):
    tokens, share = own.shape
    if share % 128:
        return columns_whole(weights, idx, tp_line(own), gain, stream, scaled)
    count = lax.axis_size("tp")
    pairs = [(own, own), tuple(beside)]

    def full(v):
        return pl.BlockSpec(v.shape, lambda i, x: (0,) * len(v.shape))

    def run(steps, begun, last):
        specs, arrays = [], []
        for step in steps:

            def owner(x, step=step):
                return jnp.clip(x[1] - step, 0, count - 1)

            specs.append(pl.BlockSpec((tokens, share), lambda i, x: (0, 0)))
            specs.append(pl.BlockSpec((weights.shape[0], share), lambda i, x, o=owner: (0, o(x))))
            arrays += [pairs[abs(step)][step < 0], weights]
            if scaled:
                specs.append(pl.BlockSpec((1, 1, share), lambda i, x, o=owner: (o(x), 0, 0)))
                arrays.append(gain)
        more = list(begun) + ([stream] if last else [])
        if last:
            outs = [jax.ShapeDtypeStruct(stream.shape, BF)]
        else:
            outs = [jax.ShapeDtypeStruct(stream.shape, F32)]
            if scaled:
                outs.append(jax.ShapeDtypeStruct((tokens, 128), F32))
        return pl.pallas_call(
            partial(columns_kernel, scaled, steps, not begun, last, share * count),
            grid_spec=pltpu.PrefetchScalarGridSpec(
                num_scalar_prefetch=1,
                grid=(1,),
                in_specs=specs + [full(v) for v in more],
                out_specs=tuple(full(v) for v in outs),
            ),
            out_shape=tuple(outs),
            compiler_params=params(50),
            cost_estimate=cost(len(steps) * 2 * 896 * 384 * 896, len(steps) * 3 * MB),
            name=("far" if last else "middle" if begun else "near") + ("_mixer" if scaled else "_output"),
        )(idx, *arrays, *more)

    steps, begun = [0, 1, -1], []
    for j in range(2, count):
        ahead = tp_step(pairs[-1])
        begun = run(steps, begun, False)
        *ahead, first = after(list(ahead) + [begun[0]], [])
        begun = [first] + list(begun[1:])
        pairs.append(tuple(ahead))
        steps = [j, -j]
    return run(steps, begun, True)[0]


def join_kernel(which_ref, mid_ref, embeds_ref, gain_ref, down_ref, act_ref, low_ref):
    owners, tokens, depth = act_ref.shape
    half = owners // 2
    squares = jnp.zeros((tokens, 1), F32)
    for i in range(owners):
        if i < half:
            part = mid_ref[i * depth : (i + 1) * depth, :].astype(F32).T
        else:
            part = embeds_ref[:, (i - half) * depth : (i - half + 1) * depth].astype(F32)
        squares = squares + jnp.sum(part * part, axis=1, keepdims=True)
        act_ref[i] = part.astype(BF)
    scale = lax.rsqrt(squares / (owners * depth) + EPSILON)
    low = jnp.zeros((tokens, down_ref.shape[2]), F32)
    for i in range(owners):
        gain = gain_ref[:, i * depth : (i + 1) * depth]
        value = (act_ref[i].astype(F32) * scale * gain).astype(BF)
        act_ref[i] = value
        low = low + dot(value, down_ref[0, i * depth : (i + 1) * depth, :])
    low_ref[...] = low.astype(BF)


def join(mid, embeds, gain, down, which, owners):
    width, tokens = mid.shape
    depth = 2 * width // owners
    rank = down.shape[2]
    return pl.pallas_call(
        join_kernel,
        grid_spec=pltpu.PrefetchScalarGridSpec(
            num_scalar_prefetch=1,
            grid=(1,),
            in_specs=[
                pl.BlockSpec((width, tokens), lambda i, a: (0, 0)),
                pl.BlockSpec((tokens, width), lambda i, a: (0, 0)),
                pl.BlockSpec((1, 2 * width), lambda i, a: (0, 0)),
                pl.BlockSpec((1, 2 * width, rank), lambda i, a: (a[0], 0, 0)),
            ],
            out_specs=(
                pl.BlockSpec((owners, tokens, depth), lambda i, a: (0, 0, 0)),
                pl.BlockSpec((tokens, rank), lambda i, a: (0, 0)),
            ),
        ),
        out_shape=(
            jax.ShapeDtypeStruct((owners, tokens, depth), BF),
            jax.ShapeDtypeStruct((tokens, rank), BF),
        ),
        compiler_params=params(48),
        cost_estimate=cost(2 * 7168 * 384 * 128, 13 * MB),
        name="join",
    )(which, mid, embeds, gain, down)


def attend_kernel(heads, size, info_ref, q_ref, kv_ref, out_ref):
    tokens, width = q_ref.shape
    length = info_ref[0]
    rows = lax.broadcasted_iota(jnp.int32, (tokens, tokens), 0)
    cols = lax.broadcasted_iota(jnp.int32, (tokens, tokens), 1)
    allowed = (cols <= rows) & (cols < length)
    spans = []
    for h in range(heads):
        left = h * size // 128 * 128
        right = min(-(-(h + 1) * size // 128) * 128, width)
        spans.append((left, right))
    done = {}
    for h, (left, right) in enumerate(spans):
        lane = lax.broadcasted_iota(jnp.int32, (tokens, right - left), 1) + left
        mine = (lane >= h * size) & (lane < (h + 1) * size)
        query = jnp.where(mine, q_ref[:, left:right].astype(F32), 0.0).astype(BF)
        scores = dot(query, kv_ref[:, left:right], NT) * size ** (-0.5)
        scores = jnp.where(allowed, scores, -1e30)
        peak = jnp.max(scores, axis=1, keepdims=True)
        expo = jnp.exp(scores - peak)
        weights = (expo / jnp.sum(expo, axis=1, keepdims=True)).astype(BF)
        mixed = dot(weights, kv_ref[:, width + left : width + right])
        mixed = jnp.where(mine, mixed, 0.0)
        for at in range(left, right, 128):
            to = min(at + 128, right)
            part = mixed[:, at - left : to - left]
            done[at] = part if at not in done else done[at] + part
    for at, value in done.items():
        out_ref[:, at : at + value.shape[1]] = value.astype(BF)


def attend(q, kv, info, heads):
    vm = pl.BlockSpec(memory_space=pltpu.VMEM)
    return pl.pallas_call(
        partial(attend_kernel, heads, HS),
        in_specs=[pl.BlockSpec(memory_space=pltpu.SMEM), vm, vm],
        out_specs=vm,
        out_shape=jax.ShapeDtypeStruct(q.shape, BF),
        compiler_params=params(40),
        cost_estimate=cost(6 * 10**9, 3 * MB),
        name="attend",
    )(info, q, kv)


def finish_kernel(rows, idx_ref, *refs):
    out_ref, all_ref = refs[-2:]
    count = len(refs) - 2
    groups = refs[0].shape[0] // rows
    for g in range(groups):
        for b, ref in enumerate(refs[:-2]):
            to = pl.multiple_of((g * count + (idx_ref[1] ^ b)) * rows, 16)
            all_ref[pl.ds(to, rows), :] = ref[g * rows : (g + 1) * rows, :]
    out_ref[...] = all_ref[...].astype(F32).T.astype(BF)


def finish(idx, parts, rows):
    count = len(parts)
    tokens = parts[0].shape[1]
    if rows % 16:
        out = jnp.zeros((parts[0].shape[0] // rows, count, rows, tokens), BF)
        for b, part in enumerate(parts):
            part = part.reshape(-1, 1, rows, tokens)
            out = lax.dynamic_update_slice_in_dim(out, part, idx[1] ^ b, 1)
        return out.reshape(-1, tokens).T
    vm = pl.BlockSpec(memory_space=pltpu.VMEM)
    width = count * parts[0].shape[0]
    return pl.pallas_call(
        partial(finish_kernel, rows),
        in_specs=[pl.BlockSpec(memory_space=pltpu.SMEM)] + [vm] * count,
        out_specs=vm,
        out_shape=jax.ShapeDtypeStruct((tokens, width), BF),
        scratch_shapes=[pltpu.VMEM((width, tokens), BF)],
        compiler_params=params(24),
        cost_estimate=cost(10**6, 2 * MB),
        name="finish",
    )(idx, *parts)


def local(
    hidden,
    embeds,
    lengths,
    live,
    adapter,
    incoming_mamba_state,
    mamba_norm_gain,
    trainer_gate_input_weight,
    trainer_step_weight,
    convolution_inner_taps,
    convolution_bc_taps,
    step_bias,
    head_decay_rate,
    direct_head_term,
    gated_norm_gain,
    trainer_mamba_output_weight,
    attention_norm_gain,
    trainer_query_key_value_weight,
    adapter_down_maps,
    adapter_up_maps,
    trainer_output_weight,
):
    tp_count, req_count = lax.axis_size("tp"), lax.axis_size("req")
    tp_index = lax.axis_index("tp").astype(jnp.int32)
    req_index = lax.axis_index("req").astype(jnp.int32)
    idx = jnp.stack([req_index, tp_index, lengths[0], live[0]])
    _, seq_len, width = hidden.shape
    heads = step_bias.shape[0]
    inner = convolution_inner_taps.shape[1]
    state_dim = convolution_bc_taps.shape[1] // 2
    rows = trainer_gate_input_weight.shape[0]

    small = trainer_step_weight.astype(BF)
    high = lax.optimization_barrier(gated_norm_gain.astype(BF))
    rest = (gated_norm_gain - high.astype(F32)).astype(BF)
    small = jnp.concatenate([small, high.reshape(rows, -1), rest.reshape(rows, -1)], axis=1)
    used, each = trainer_step_weight.shape[1], inner // rows
    small = jnp.pad(small, ((0, 0), (0, 256 - small.shape[1])))
    zx_send = prepare_input(idx, trainer_gate_input_weight.transpose(1, 0, 2), small, tp_count)
    zx_received = tp_send(zx_send)
    out_server = gather_rows(trainer_mamba_output_weight.astype(BF).T)
    q_send, kv_send = prepare(
        trainer_query_key_value_weight.transpose(1, 0, 2), tp_count, [(0,), (1, 2)]
    )
    normed_in = norm(hidden[0], mamba_norm_gain[None, :], req_count)
    per_head = head_rows(step_bias, head_decay_rate, direct_head_term, heads, inner)
    zx_own = tp_place(idx, zx_received)

    stream_t = hidden[0].T.reshape(req_count, tp_count, rows, seq_len)
    stream_t = lax.dynamic_index_in_dim(stream_t, tp_index, 1, keepdims=False)
    stream_t = stream_t.reshape(req_count * rows, seq_len)
    ups = lax.dynamic_index_in_dim(adapter_up_maps, adapter[0], 0, keepdims=False)
    ups = [ups[:, 0], ups[:, 1:].reshape(ups.shape[0], -1)]
    o_own = trainer_output_weight.astype(BF).T

    early = [normed_in, q_send, kv_send, stream_t, o_own] + ups + per_head
    zx_own, *early = after([zx_own] + early, [])
    normed_in, q_send, kv_send, stream_t, o_own = early[:5]
    ups, per_head = early[5:7], early[7:]
    zx_gather = Gather(zx_own)
    zx_first = zx_gather.first()
    q_send, zx_gather.core = after([q_send, zx_gather.core], [])
    q_own = tp_trade(q_send)
    gain_all = zx_own.reshape(tp_count, rows, -1)[:, :, 2 * inner + used :].astype(F32)
    gain_all = (gain_all[:, :, :each] + gain_all[:, :, each : 2 * each]).reshape(tp_count, 1, inner)

    held = after(zx_first + [kv_send, q_own], [gain_all])
    if req_count == 8:
        zx_gather.refresh(["px", "py"], held[:2])
    kv_send, q_own = held[-2:]
    kv_own = tp_trade(kv_send)
    zx_second = zx_gather.second()
    q_own, *_ = after([q_own], [out_server])
    q_server = gather_rows(q_own)
    zx_gather.third()

    zx = pieces_matmul(normed_in, zx_gather)
    info = jnp.stack([lengths[0], tp_index * heads])
    raw, final = run_scan(
        zx, info, convolution_inner_taps, convolution_bc_taps, per_head, heads, inner, state_dim
    )
    beside = tp_step((raw, raw))
    kv_own, *beside = after([kv_own, *beside], [])
    kv_server = gather_rows(kv_own)
    mid_own = columns(out_server, idx, raw, beside, gain_all, stream_t, True)
    mid = tp_stack(tp_line(mid_own), tp_index)
    mid = mid.reshape(tp_count, req_count, rows, seq_len).transpose(1, 0, 2, 3)
    mid = mid.reshape(width, seq_len)
    act, low = join(mid, embeds[0], attention_norm_gain[None, :], adapter_down_maps, adapter, 4)
    queries = rows_matmul(act, q_server, low, ups[0])
    o_own, kv_server = after([o_own, kv_server], [queries])
    o_server = gather_rows(o_own)
    keys_values = rows_matmul(act, kv_server, low, ups[1])
    attended = attend(queries, keys_values, lengths, queries.shape[1] // HS)
    result = columns(o_server, idx, attended, tp_step((attended, attended)), gain_all, mid_own, False)
    result = tp_send(by_xor(result.reshape(tp_count, -1, seq_len)))
    result = finish(idx, result, rows)
    final = final.reshape((1, heads, inner // heads, state_dim))
    state = jnp.where((live > 0)[:, None, None, None], final, incoming_mamba_state)
    return (result[None], state)


def solution(mesh):
    placed = (
        P("req", None, None),
        P("req", None, None),
        P("req"),
        P("req"),
        P("req"),
        P("req", "tp", None, None),
        P(),
        P(("req", "tp"), None, None),
        P(("req", "tp"), None),
        P(None, "tp"),
        P(),
        P("tp"),
        P("tp"),
        P("tp"),
        P("tp"),
        P(None, ("req", "tp")),
        P(),
        P(("req", "tp"), None, None),
        P(),
        P(None, None, None, "tp"),
        P(None, ("req", "tp")),
    )
    return jax.shard_map(
        local,
        mesh=mesh,
        in_specs=placed,
        out_specs=(P("req", None, "tp"), P("req", "tp", None, None)),
        check_vma=False,
    )
```

```python
from functools import partial

import jax
import jax.numpy as jnp
from jax import lax
from jax.experimental import pallas as pl
from jax.experimental.pallas import tpu as pltpu
from jax.sharding import PartitionSpec as P

HS = 224
EPSILON = 1e-05
HIGHEST = lax.Precision.HIGHEST
BF = jnp.bfloat16
F32 = jnp.float32
NT = (((1,), (1,)), ((), ()))
NN = (((1,), (0,)), ((), ()))
TN = (((0,), (0,)), ((), ()))
MB = 1 << 20


def dot(a, b, dims=NN, precision=None):
    return lax.dot_general(a, b, dims, precision=precision, preferred_element_type=F32)


def params(mb):
    return pltpu.CompilerParams(vmem_limit_bytes=mb * MB)


def cost(flops, nbytes):
    return pl.CostEstimate(flops=flops, bytes_accessed=nbytes, transcendentals=0)


def exchange(value, axis, bits):
    count = lax.axis_size(axis)
    return lax.ppermute(value, axis, [(i, i ^ bits) for i in range(count)])


def after(values, waited):
    held = lax.optimization_barrier(tuple(values) + tuple(waited))
    return list(held[: len(values)])


def prepare_input_kernel(idx_ref, w_ref, small_ref, *outs):
    tp = idx_ref[1]
    count = len(outs)
    share = w_ref.shape[2] // count
    for k in range(2):
        for t in range(count):
            piece = w_ref[k, :, t * share : (t + 1) * share].astype(BF)
            for b in range(count):

                @pl.when(tp ^ b == t)
                def _():
                    outs[b][:, k * share : (k + 1) * share] = piece

    for b in range(count):
        outs[b][:, 2 * share :] = small_ref[...]


def prepare_input(idx, weight, small, count):
    _, rows, width = weight.shape
    cols = 2 * width // count + small.shape[1]
    vm = pl.BlockSpec(memory_space=pltpu.VMEM)
    outs = pl.pallas_call(
        prepare_input_kernel,
        in_specs=[pl.BlockSpec(memory_space=pltpu.SMEM), vm, vm],
        out_specs=(vm,) * count,
        out_shape=(jax.ShapeDtypeStruct((rows, cols), BF),) * count,
        compiler_params=params(32),
        cost_estimate=cost(10**6, 6 * MB),
        name="prepare_input",
    )(idx, weight, small)
    return list(outs)


def prepare_kernel(groups, w_ref, *outs):
    for out_ref, parts in zip(outs, groups):
        count = out_ref.shape[0]
        share = w_ref.shape[2] // count
        for j, k in enumerate(parts):
            for t in range(count):
                piece = w_ref[k, :, t * share : (t + 1) * share].astype(BF)
                out_ref[t, :, j * share : (j + 1) * share] = piece


def prepare(weight, count, groups):
    parts, rows, width = weight.shape
    share = width // count
    block = rows // 2 if rows % 32 == 0 else rows
    shapes = [jax.ShapeDtypeStruct((count, rows, share * len(g)), BF) for g in groups]
    return pl.pallas_call(
        partial(prepare_kernel, groups),
        grid=(rows // block,),
        in_specs=[pl.BlockSpec((parts, block, width), lambda i: (0, i, 0))],
        out_specs=tuple(pl.BlockSpec((count, block, v.shape[2]), lambda i: (0, i, 0)) for v in shapes),
        out_shape=tuple(shapes),
        compiler_params=params(40),
        cost_estimate=cost(10**6, parts * rows * width * 6),
        name="prepare",
    )(weight)


def tp_trade(slices):
    out = lax.all_to_all(slices, "tp", split_axis=0, concat_axis=0, tiled=True)
    return out.reshape(-1, slices.shape[2])


def norm_kernel(x_ref, gain_ref, out_ref):
    depth = out_ref.shape[2]
    x = x_ref[...].astype(F32)
    scale = lax.rsqrt(jnp.mean(x * x, axis=1, keepdims=True) + EPSILON)
    for i in range(out_ref.shape[0]):
        span = slice(i * depth, (i + 1) * depth)
        out_ref[i] = (x_ref[:, span].astype(F32) * scale * gain_ref[:, span]).astype(BF)


def norm(x, gain, owners):
    tokens, width = x.shape
    vm = pl.BlockSpec(memory_space=pltpu.VMEM)
    return pl.pallas_call(
        norm_kernel,
        in_specs=[vm, vm],
        out_specs=vm,
        out_shape=jax.ShapeDtypeStruct((owners, tokens, width // owners), BF),
        compiler_params=params(32),
        cost_estimate=cost(10**7, 6 * MB),
        name="norm",
    )(x, gain)


def tp_send(pieces):
    return [pieces[0]] + [exchange(p, "tp", b) for b, p in enumerate(pieces) if b]


def tp_step(pair):
    count = lax.axis_size("tp")
    return (
        lax.ppermute(pair[0], "tp", [(i, i + 1) for i in range(count - 1)]),
        lax.ppermute(pair[1], "tp", [(i + 1, i) for i in range(count - 1)]),
    )


def tp_line(own):
    pairs = [(own, own)]
    for _ in range(lax.axis_size("tp") - 1):
        pairs.append(tp_step(pairs[-1]))
    return pairs


def tp_stack(pairs, tp_index):
    count = len(pairs)
    out = jnp.zeros((count,) + pairs[0][0].shape, pairs[0][0].dtype)
    out = lax.dynamic_update_index_in_dim(out, pairs[0][0], tp_index, 0)
    for j in range(1, count):
        piece = jnp.where(tp_index >= j, pairs[j][0], pairs[count - j][1])
        out = lax.dynamic_update_index_in_dim(out, piece, (tp_index - j) % count, 0)
    return out


def by_xor(slices):
    me = lax.axis_index("tp")
    return [
        lax.dynamic_index_in_dim(slices, me ^ b, 0, keepdims=False) for b in range(slices.shape[0])
    ]


def place_kernel(idx_ref, *refs):
    out_ref = refs[-1]
    rows = refs[0].shape[0]
    for b, ref in enumerate(refs[:-1]):
        out_ref[pl.ds(pl.multiple_of((idx_ref[1] ^ b) * rows, 16), rows), :] = ref[...]


def tp_place(idx, received):
    count = len(received)
    rows, cols = received[0].shape
    if rows % 16:
        out = jnp.zeros((count, rows, cols), BF)
        for b, piece in enumerate(received):
            out = lax.dynamic_update_index_in_dim(out, piece, idx[1] ^ b, 0)
        return out.reshape(count * rows, cols)
    vm = pl.BlockSpec(memory_space=pltpu.VMEM)
    return pl.pallas_call(
        place_kernel,
        in_specs=[pl.BlockSpec(memory_space=pltpu.SMEM)] + [vm] * count,
        out_specs=vm,
        out_shape=jax.ShapeDtypeStruct((count * rows, cols), BF),
        compiler_params=params(24),
        cost_estimate=cost(10**6, 2 * count * rows * cols * 2),
        name="place",
    )(idx, *received)


def gather_rows(piece):
    return lax.all_gather(piece, "req", axis=0, tiled=True)


class Gather:
    def __init__(self, own):
        self.own = own
        self.count = lax.axis_size("req")
        self.pieces = [(0, 0, own)]

    def first(self):
        own = self.own
        self.core = exchange(own, "req", 1)
        if self.count == 8:
            self.px, self.py = exchange(own, "req", 2), exchange(own, "req", 4)
            return [self.px, self.py]
        moved = [(0, own)]
        bit = 2
        while bit < self.count:
            moved = moved + [(at ^ bit, exchange(v, "req", bit)) for at, v in moved]
            bit *= 2
        self.moved = moved
        return [v for _, v in moved[1:]]

    def second(self):
        if self.count != 8:
            self.pieces = [(at, 0, v) for at, v in self.moved]
            self.pieces += [(at ^ 1, 0, exchange(v, "req", 1)) for at, v in self.moved[1:]]
            self.pieces.append((1, 0, self.core))
            return []
        half = -(-self.own.shape[0] // 32) * 16
        self.half = half
        self.d0 = exchange(self.py[:half], "req", 2)
        self.d1 = exchange(self.px[half:], "req", 4)
        self.pieces.append((1, 0, self.core))
        self.pieces += [(2, 0, self.px), (4, 0, self.py)]
        self.pieces += [(3, 0, exchange(self.px, "req", 1)), (5, 0, exchange(self.py, "req", 1))]
        return [self.d0, self.d1]

    def third(self):
        if self.count != 8:
            return
        self.pieces += [(6, 0, self.d0), (6, self.half, self.d1)]
        self.pieces += [
            (7, 0, exchange(self.d0, "req", 1)),
            (7, self.half, exchange(self.d1, "req", 1)),
        ]

    def refresh(self, names, values):
        for name, value in zip(names, values):
            setattr(self, name, value)


def pieces_kernel(places, req_ref, act_ref, *refs):
    count = len(places)
    out_ref, buf_ref, acc_ref, sems = refs[count:]
    me = req_ref[0]
    width = acc_ref.shape[1]
    starts = []
    total = 0
    for _, _, rows in places:
        starts.append(total)
        total += rows

    def copy(i):
        rows = places[i][2]
        return pltpu.make_async_copy(
            refs[i], buf_ref.at[starts[i] : starts[i] + rows, :], sems.at[i]
        )

    for i in range(count):
        copy(i).start()
    for i, (at, low, rows) in enumerate(places):
        copy(i).wait()
        a = act_ref[me ^ at][:, low : low + rows]
        for left in range(0, width, 512):
            span = slice(left, min(left + 512, width))
            part = dot(a, buf_ref[starts[i] : starts[i] + rows, span])
            if i:
                part = part + acc_ref[:, span]
            if i < count - 1:
                acc_ref[:, span] = part
            else:
                out_ref[:, span] = part.astype(BF)


def pieces_matmul(act, gathered):
    owners, tokens, depth = act.shape
    width = gathered.own.shape[1]
    me = lax.axis_index("req").astype(jnp.int32).reshape(1)
    places = [(at, first, v.shape[0]) for at, first, v in gathered.pieces]
    arrays = [v for _, _, v in gathered.pieces]
    vm = pl.BlockSpec(memory_space=pltpu.VMEM)
    return pl.pallas_call(
        partial(pieces_kernel, places),
        in_specs=[pl.BlockSpec(memory_space=pltpu.SMEM), vm]
        + [pl.BlockSpec(memory_space=pl.ANY)] * len(arrays),
        out_specs=vm,
        out_shape=jax.ShapeDtypeStruct((tokens, width), BF),
        scratch_shapes=[
            pltpu.VMEM((owners * depth, width), BF),
            pltpu.VMEM((tokens, width), F32),
            pltpu.SemaphoreType.DMA((len(arrays),)),
        ],
        compiler_params=params(40),
        cost_estimate=cost(2 * owners * tokens * depth * width, owners * depth * width * 2),
        name="zx",
    )(me, act, *arrays)


def rows_kernel(act_ref, w_ref, low_ref, up_ref, out_ref, acc_ref):
    step = pl.program_id(0)
    part = dot(act_ref[0], w_ref[...])

    @pl.when(step == 0)
    def _():
        acc_ref[...] = part + dot(low_ref[...], up_ref[...])

    @pl.when((step > 0) & (step < pl.num_programs(0) - 1))
    def _():
        acc_ref[...] += part

    @pl.when(step == pl.num_programs(0) - 1)
    def _():
        out_ref[...] = (acc_ref[...] + part).astype(BF)


def rows_matmul(act, weight, low, up):
    owners, tokens, depth = act.shape
    width = weight.shape[1]
    return pl.pallas_call(
        rows_kernel,
        grid=(owners,),
        in_specs=[
            pl.BlockSpec((1, tokens, depth), lambda i: (i, 0, 0)),
            pl.BlockSpec((depth, width), lambda i: (i, 0)),
            pl.BlockSpec(low.shape, lambda i: (0, 0)),
            pl.BlockSpec(up.shape, lambda i: (0, 0)),
        ],
        out_specs=pl.BlockSpec((tokens, width), lambda i: (0, 0)),
        out_shape=jax.ShapeDtypeStruct((tokens, width), BF),
        scratch_shapes=[pltpu.VMEM((tokens, width), F32)],
        compiler_params=params(58),
        cost_estimate=cost(2 * owners * tokens * depth * width, owners * depth * width * 2),
        name="qkv",
    )(act, weight, low, up)


def scan_kernel(
    heads, inner, state_dim, chunk, info_ref, zx_ref, taps_ref, bc_taps_ref, bias_ref, bias_t_ref,
    rate_ref, rate_t_ref, direct_ref, out_ref, final_ref, pad_ref, bcpad_ref, conv_ref, bc_ref,
):
    tokens = out_ref.shape[0]
    head_dim = inner // heads
    length, first_head = info_ref[0], info_ref[1]
    width = taps_ref.shape[0]
    pad_ref[0:8, :] = jnp.zeros((8, inner), F32)
    pad_ref[8:, :] = zx_ref[:, inner : 2 * inner].astype(F32)
    bcpad_ref[0:8, :] = jnp.zeros((8, 2 * state_dim), F32)
    bcpad_ref[8:, :] = zx_ref[:, 2 * inner : 2 * inner + 2 * state_dim].astype(F32)
    for base in range(0, tokens, chunk):
        x = jnp.zeros((chunk, inner), F32)
        b = jnp.zeros((chunk, 2 * state_dim), F32)
        for k in range(width):
            low = base + 8 - (width - 1) + k
            x = x + taps_ref[k : k + 1, :] * pad_ref[low : low + chunk, :]
            b = b + bc_taps_ref[k : k + 1, :] * bcpad_ref[low : low + chunk, :]
        conv_ref[base : base + chunk, :] = x * jax.nn.sigmoid(x)
        bc_ref[base : base + chunk, :] = b * jax.nn.sigmoid(b)

    def softplus(v):
        return jnp.maximum(v, 0.0) + jnp.log1p(jnp.exp(-jnp.abs(v)))

    raw = zx_ref[:, 2 * inner + 2 * state_dim :]
    lanes = raw.shape[1]
    pick = (
        lax.broadcasted_iota(jnp.int32, (lanes, 128), 0)
        == lax.broadcasted_iota(jnp.int32, (lanes, 128), 1) + first_head
    ).astype(F32).astype(BF)
    pick_t = (
        lax.broadcasted_iota(jnp.int32, (16, lanes), 1)
        == lax.broadcasted_iota(jnp.int32, (16, lanes), 0) + first_head
    ).astype(F32).astype(BF)
    valid = lax.broadcasted_iota(jnp.int32, (tokens, 128), 0) < length
    valid_t = lax.broadcasted_iota(jnp.int32, (16, tokens), 1) < length
    steps = jnp.where(valid, softplus(dot(raw, pick) + bias_ref[...]), 0.0)
    steps_t = jnp.where(valid_t, softplus(dot(pick_t, raw, NT) + bias_t_ref[...]), 0.0)
    logs = -steps * rate_ref[...]
    logs_t = -steps_t * rate_t_ref[...]
    rows = lax.broadcasted_iota(jnp.int32, (chunk, chunk), 0)
    cols = lax.broadcasted_iota(jnp.int32, (chunk, chunk), 1)
    lower = rows >= cols
    tri = lower.astype(F32)
    tri_t = (rows <= cols).astype(F32)
    spread = (
        lax.broadcasted_iota(jnp.int32, (128, inner), 1) // head_dim
        == lax.broadcasted_iota(jnp.int32, (128, inner), 0)
    ).astype(F32)
    state = jnp.zeros((state_dim, inner), F32)
    for base in range(0, tokens, chunk):
        span = slice(base, base + chunk)
        x = conv_ref[span, :]
        bc = bc_ref[span, :]
        b_rows = bc[:, :state_dim].astype(BF)
        c_rows = bc[:, state_dim:].astype(BF)
        cumul = dot(tri, logs[span, :], precision=HIGHEST)
        cumul_t = dot(logs_t[:, span], tri_t, precision=HIGHEST)
        last = cumul[chunk - 1 : chunk, :]
        near = dot(c_rows, b_rows, NT)
        near = jnp.where(lower, near, 0.0)
        grown = dot(jnp.exp(cumul), spread, precision=HIGHEST)
        x_dt = x * dot(steps[span, :], spread, precision=HIGHEST)
        tail = dot(jnp.exp(last - cumul), spread, precision=HIGHEST)
        carried = dot(c_rows, state.astype(BF)) * grown
        x_dt_b = x_dt.astype(BF)
        direct = direct_ref[...] * x + carried
        gate = zx_ref[span, :inner].astype(F32)
        gate = gate * jax.nn.sigmoid(gate)
        per = 128 // head_dim
        for tile in range(pl.cdiv(heads, per)):
            left, right = tile * 128, min(tile * 128 + 128, inner)
            lane = lax.broadcasted_iota(jnp.int32, (chunk, right - left), 1)
            within = jnp.zeros((chunk, right - left), F32)
            for h in range(tile * per, min(tile * per + per, heads)):
                gap = cumul[:, h : h + 1] - cumul_t[h : h + 1, :]
                gap = jnp.where(lower, gap, -1e30)
                weights = (near * jnp.exp(gap)).astype(BF)
                part = dot(weights, x_dt_b[:, left:right])
                mine = lane // head_dim == h - tile * per
                within = jnp.where(mine, part, within)
            y = (within + direct[:, left:right]) * gate[:, left:right]
            out_ref[span, left:right] = y.astype(BF)
        fresh = dot(b_rows, (x_dt * tail).astype(BF), TN)
        kept = dot(jnp.broadcast_to(jnp.exp(last), (8, 128)), spread, precision=HIGHEST)[0:1, :]
        state = state * kept + fresh
    final_ref[...] = state.T


def head_rows(bias, rate, direct, heads, inner):
    def padded(v):
        return [
            jnp.pad(v[None, :], ((0, 0), (0, 128 - heads))),
            jnp.pad(v[:, None], ((0, 16 - heads), (0, 0))),
        ]

    return padded(bias) + padded(rate) + [jnp.repeat(direct, inner // heads)[None, :]]


def run_scan(zx, info, taps, bc_taps, per_head, heads, inner, state_dim):
    tokens = zx.shape[0]
    vm = pl.BlockSpec(memory_space=pltpu.VMEM)
    return pl.pallas_call(
        partial(scan_kernel, heads, inner, state_dim, 128),
        in_specs=[pl.BlockSpec(memory_space=pltpu.SMEM)] + [vm] * 8,
        out_specs=(vm, vm),
        out_shape=(
            jax.ShapeDtypeStruct((tokens, inner), BF),
            jax.ShapeDtypeStruct((inner, state_dim), F32),
        ),
        scratch_shapes=[
            pltpu.VMEM((tokens + 8, inner), F32),
            pltpu.VMEM((tokens + 8, 2 * state_dim), F32),
            pltpu.VMEM((tokens, inner), F32),
            pltpu.VMEM((tokens, 2 * state_dim), F32),
        ],
        compiler_params=params(40),
        cost_estimate=cost(6 * 10**9, 4 * MB),
        name="scan",
    )(info, zx, taps, bc_taps, *per_head)


def columns_part(scaled, steps, idx_ref, refs):
    each = 3 if scaled else 2
    squares = total = None
    for i, step in enumerate(steps):
        act_ref, w_ref = refs[each * i], refs[each * i + 1]
        act = act_ref[...]
        if scaled:
            raw = act.astype(F32)
            square = jnp.sum(raw * raw, axis=1, keepdims=True)
            squares = square if squares is None else squares + square
            act = (raw * refs[each * i + 2][0]).astype(BF)
        part = dot(w_ref[...], act, NT)
        total = part if total is None else total + part
    return total, squares


def columns_kernel(scaled, steps, begin, last, denominator, idx_ref, *refs):
    count = (3 if scaled else 2) * len(steps)
    total, squares = columns_part(scaled, steps, idx_ref, refs)
    rest = list(refs[count:])
    if not begin:
        total = total + rest.pop(0)[...]
        if scaled:
            squares = squares + rest.pop(0)[...]
    if not last:
        rest[0][...] = total
        if scaled:
            rest[1][...] = jnp.broadcast_to(squares, rest[1].shape)
        return
    stream_ref, out_ref = rest
    if scaled:
        scale = lax.rsqrt(squares / denominator + EPSILON)
        total = total * scale.T[0:1, :]
    total = stream_ref[...].astype(F32) + total
    if not scaled:
        place = lax.broadcasted_iota(jnp.int32, total.shape, 1)
        keep = place < jnp.where(idx_ref[3] > 0, idx_ref[2], 0)
        total = jnp.where(keep, total, 0.0)
    out_ref[...] = total.astype(BF)


def columns_whole(weights, idx, pairs, gain, stream, scaled):
    acts = tp_stack(pairs, idx[1])
    count, tokens, share = acts.shape
    raw = acts.astype(F32)
    if scaled:
        acts = (raw * gain).astype(BF)
    flat = acts.transpose(1, 0, 2).reshape(tokens, count * share)
    total = dot(weights, flat, NT)
    if scaled:
        squares = jnp.sum(raw * raw, axis=(0, 2)) / (count * share)
        total = total * lax.rsqrt(squares + EPSILON)[None, :]
    total = stream.astype(F32) + total
    if not scaled:
        total = jnp.where(jnp.arange(tokens)[None, :] < idx[2] * (idx[3] > 0), total, 0.0)
    return total.astype(BF)


def columns(weights, idx, own, beside, gain, stream, scaled):
    tokens, share = own.shape
    if share % 128:
        return columns_whole(weights, idx, tp_line(own), gain, stream, scaled)
    count = lax.axis_size("tp")
    pairs = [(own, own), tuple(beside)]

    def full(v):
        return pl.BlockSpec(v.shape, lambda i, x: (0,) * len(v.shape))

    def run(steps, begun, last):
        specs, arrays = [], []
        for step in steps:

            def owner(x, step=step):
                return jnp.clip(x[1] - step, 0, count - 1)

            specs.append(pl.BlockSpec((tokens, share), lambda i, x: (0, 0)))
            specs.append(pl.BlockSpec((weights.shape[0], share), lambda i, x, o=owner: (0, o(x))))
            arrays += [pairs[abs(step)][step < 0], weights]
            if scaled:
                specs.append(pl.BlockSpec((1, 1, share), lambda i, x, o=owner: (o(x), 0, 0)))
                arrays.append(gain)
        more = list(begun) + ([stream] if last else [])
        if last:
            outs = [jax.ShapeDtypeStruct(stream.shape, BF)]
        else:
            outs = [jax.ShapeDtypeStruct(stream.shape, F32)]
            if scaled:
                outs.append(jax.ShapeDtypeStruct((tokens, 128), F32))
        return pl.pallas_call(
            partial(columns_kernel, scaled, steps, not begun, last, share * count),
            grid_spec=pltpu.PrefetchScalarGridSpec(
                num_scalar_prefetch=1,
                grid=(1,),
                in_specs=specs + [full(v) for v in more],
                out_specs=tuple(full(v) for v in outs),
            ),
            out_shape=tuple(outs),
            compiler_params=params(50),
            cost_estimate=cost(len(steps) * 2 * 896 * 384 * 896, len(steps) * 3 * MB),
            name=("far" if last else "middle" if begun else "near") + ("_mixer" if scaled else "_output"),
        )(idx, *arrays, *more)

    steps, begun = [0, 1, -1], []
    for j in range(2, count):
        ahead = tp_step(pairs[-1])
        begun = run(steps, begun, False)
        *ahead, first = after(list(ahead) + [begun[0]], [])
        begun = [first] + list(begun[1:])
        pairs.append(tuple(ahead))
        steps = [j, -j]
    return run(steps, begun, True)[0]


def join_kernel(which_ref, mid_ref, embeds_ref, gain_ref, down_ref, act_ref, low_ref):
    owners, tokens, depth = act_ref.shape
    half = owners // 2
    squares = jnp.zeros((tokens, 1), F32)
    for i in range(owners):
        if i < half:
            part = mid_ref[i * depth : (i + 1) * depth, :].astype(F32).T
        else:
            part = embeds_ref[:, (i - half) * depth : (i - half + 1) * depth].astype(F32)
        squares = squares + jnp.sum(part * part, axis=1, keepdims=True)
        act_ref[i] = part.astype(BF)
    scale = lax.rsqrt(squares / (owners * depth) + EPSILON)
    low = jnp.zeros((tokens, down_ref.shape[2]), F32)
    for i in range(owners):
        gain = gain_ref[:, i * depth : (i + 1) * depth]
        value = (act_ref[i].astype(F32) * scale * gain).astype(BF)
        act_ref[i] = value
        low = low + dot(value, down_ref[0, i * depth : (i + 1) * depth, :])
    low_ref[...] = low.astype(BF)


def join(mid, embeds, gain, down, which, owners):
    width, tokens = mid.shape
    depth = 2 * width // owners
    rank = down.shape[2]
    return pl.pallas_call(
        join_kernel,
        grid_spec=pltpu.PrefetchScalarGridSpec(
            num_scalar_prefetch=1,
            grid=(1,),
            in_specs=[
                pl.BlockSpec((width, tokens), lambda i, a: (0, 0)),
                pl.BlockSpec((tokens, width), lambda i, a: (0, 0)),
                pl.BlockSpec((1, 2 * width), lambda i, a: (0, 0)),
                pl.BlockSpec((1, 2 * width, rank), lambda i, a: (a[0], 0, 0)),
            ],
            out_specs=(
                pl.BlockSpec((owners, tokens, depth), lambda i, a: (0, 0, 0)),
                pl.BlockSpec((tokens, rank), lambda i, a: (0, 0)),
            ),
        ),
        out_shape=(
            jax.ShapeDtypeStruct((owners, tokens, depth), BF),
            jax.ShapeDtypeStruct((tokens, rank), BF),
        ),
        compiler_params=params(48),
        cost_estimate=cost(2 * 7168 * 384 * 128, 13 * MB),
        name="join",
    )(which, mid, embeds, gain, down)


def attend_kernel(heads, size, info_ref, q_ref, kv_ref, out_ref):
    tokens, width = q_ref.shape
    length = info_ref[0]
    rows = lax.broadcasted_iota(jnp.int32, (tokens, tokens), 0)
    cols = lax.broadcasted_iota(jnp.int32, (tokens, tokens), 1)
    allowed = (cols <= rows) & (cols < length)
    spans = []
    for h in range(heads):
        left = h * size // 128 * 128
        right = min(-(-(h + 1) * size // 128) * 128, width)
        spans.append((left, right))
    done = {}
    for h, (left, right) in enumerate(spans):
        lane = lax.broadcasted_iota(jnp.int32, (tokens, right - left), 1) + left
        mine = (lane >= h * size) & (lane < (h + 1) * size)
        query = jnp.where(mine, q_ref[:, left:right].astype(F32), 0.0).astype(BF)
        scores = dot(query, kv_ref[:, left:right], NT) * size ** (-0.5)
        scores = jnp.where(allowed, scores, -1e30)
        peak = jnp.max(scores, axis=1, keepdims=True)
        expo = jnp.exp(scores - peak)
        weights = (expo / jnp.sum(expo, axis=1, keepdims=True)).astype(BF)
        mixed = dot(weights, kv_ref[:, width + left : width + right])
        mixed = jnp.where(mine, mixed, 0.0)
        for at in range(left, right, 128):
            to = min(at + 128, right)
            part = mixed[:, at - left : to - left]
            done[at] = part if at not in done else done[at] + part
    for at, value in done.items():
        out_ref[:, at : at + value.shape[1]] = value.astype(BF)


def attend(q, kv, info, heads):
    vm = pl.BlockSpec(memory_space=pltpu.VMEM)
    return pl.pallas_call(
        partial(attend_kernel, heads, HS),
        in_specs=[pl.BlockSpec(memory_space=pltpu.SMEM), vm, vm],
        out_specs=vm,
        out_shape=jax.ShapeDtypeStruct(q.shape, BF),
        compiler_params=params(40),
        cost_estimate=cost(6 * 10**9, 3 * MB),
        name="attend",
    )(info, q, kv)


def finish_kernel(rows, idx_ref, *refs):
    out_ref, all_ref = refs[-2:]
    count = len(refs) - 2
    groups = refs[0].shape[0] // rows
    for g in range(groups):
        for b, ref in enumerate(refs[:-2]):
            to = pl.multiple_of((g * count + (idx_ref[1] ^ b)) * rows, 16)
            all_ref[pl.ds(to, rows), :] = ref[g * rows : (g + 1) * rows, :]
    out_ref[...] = all_ref[...].astype(F32).T.astype(BF)


def finish(idx, parts, rows):
    count = len(parts)
    tokens = parts[0].shape[1]
    if rows % 16:
        out = jnp.zeros((parts[0].shape[0] // rows, count, rows, tokens), BF)
        for b, part in enumerate(parts):
            part = part.reshape(-1, 1, rows, tokens)
            out = lax.dynamic_update_slice_in_dim(out, part, idx[1] ^ b, 1)
        return out.reshape(-1, tokens).T
    vm = pl.BlockSpec(memory_space=pltpu.VMEM)
    width = count * parts[0].shape[0]
    return pl.pallas_call(
        partial(finish_kernel, rows),
        in_specs=[pl.BlockSpec(memory_space=pltpu.SMEM)] + [vm] * count,
        out_specs=vm,
        out_shape=jax.ShapeDtypeStruct((tokens, width), BF),
        scratch_shapes=[pltpu.VMEM((width, tokens), BF)],
        compiler_params=params(24),
        cost_estimate=cost(10**6, 2 * MB),
        name="finish",
    )(idx, *parts)


def local(
    hidden,
    embeds,
    lengths,
    live,
    adapter,
    incoming_mamba_state,
    mamba_norm_gain,
    trainer_gate_input_weight,
    trainer_step_weight,
    convolution_inner_taps,
    convolution_bc_taps,
    step_bias,
    head_decay_rate,
    direct_head_term,
    gated_norm_gain,
    trainer_mamba_output_weight,
    attention_norm_gain,
    trainer_query_key_value_weight,
    adapter_down_maps,
    adapter_up_maps,
    trainer_output_weight,
):
    tp_count, req_count = lax.axis_size("tp"), lax.axis_size("req")
    tp_index = lax.axis_index("tp").astype(jnp.int32)
    req_index = lax.axis_index("req").astype(jnp.int32)
    idx = jnp.stack([req_index, tp_index, lengths[0], live[0]])
    _, seq_len, width = hidden.shape
    heads = step_bias.shape[0]
    inner = convolution_inner_taps.shape[1]
    state_dim = convolution_bc_taps.shape[1] // 2
    rows = trainer_gate_input_weight.shape[0]

    small = trainer_step_weight.astype(BF)
    high = lax.optimization_barrier(gated_norm_gain.astype(BF))
    rest = (gated_norm_gain - high.astype(F32)).astype(BF)
    small = jnp.concatenate([small, high.reshape(rows, -1), rest.reshape(rows, -1)], axis=1)
    used, each = trainer_step_weight.shape[1], inner // rows
    small = jnp.pad(small, ((0, 0), (0, 256 - small.shape[1])))
    zx_send = prepare_input(idx, trainer_gate_input_weight.transpose(1, 0, 2), small, tp_count)
    zx_received = tp_send(zx_send)
    out_server = gather_rows(trainer_mamba_output_weight.astype(BF).T)
    q_send, kv_send = prepare(
        trainer_query_key_value_weight.transpose(1, 0, 2), tp_count, [(0,), (1, 2)]
    )
    normed_in = norm(hidden[0], mamba_norm_gain[None, :], req_count)
    per_head = head_rows(step_bias, head_decay_rate, direct_head_term, heads, inner)
    zx_own = tp_place(idx, zx_received)

    stream_t = hidden[0].T.reshape(req_count, tp_count, rows, seq_len)
    stream_t = lax.dynamic_index_in_dim(stream_t, tp_index, 1, keepdims=False)
    stream_t = stream_t.reshape(req_count * rows, seq_len)
    ups = lax.dynamic_index_in_dim(adapter_up_maps, adapter[0], 0, keepdims=False)
    ups = [ups[:, 0], ups[:, 1:].reshape(ups.shape[0], -1)]
    o_own = trainer_output_weight.astype(BF).T

    early = [normed_in, q_send, kv_send, stream_t, o_own] + ups + per_head
    zx_own, *early = after([zx_own] + early, [])
    normed_in, q_send, kv_send, stream_t, o_own = early[:5]
    ups, per_head = early[5:7], early[7:]
    zx_gather = Gather(zx_own)
    zx_first = zx_gather.first()
    q_own = tp_trade(q_send)
    gain_all = zx_own.reshape(tp_count, rows, -1)[:, :, 2 * inner + used :].astype(F32)
    gain_all = (gain_all[:, :, :each] + gain_all[:, :, each : 2 * each]).reshape(tp_count, 1, inner)

    held = after(zx_first + [kv_send, q_own], [gain_all])
    if req_count == 8:
        zx_gather.refresh(["px", "py"], held[:2])
    kv_send, q_own = held[-2:]
    kv_own = tp_trade(kv_send)
    zx_second = zx_gather.second()
    q_own, *_ = after([q_own], [out_server])
    q_server = gather_rows(q_own)
    zx_gather.third()

    zx = pieces_matmul(normed_in, zx_gather)
    info = jnp.stack([lengths[0], tp_index * heads])
    raw, final = run_scan(
        zx, info, convolution_inner_taps, convolution_bc_taps, per_head, heads, inner, state_dim
    )
    beside = tp_step((raw, raw))
    kv_own, *beside = after([kv_own, *beside], [])
    kv_server = gather_rows(kv_own)
    mid_own = columns(out_server, idx, raw, beside, gain_all, stream_t, True)
    mid = tp_stack(tp_line(mid_own), tp_index)
    mid = mid.reshape(tp_count, req_count, rows, seq_len).transpose(1, 0, 2, 3)
    mid = mid.reshape(width, seq_len)
    act, low = join(mid, embeds[0], attention_norm_gain[None, :], adapter_down_maps, adapter, 4)
    queries = rows_matmul(act, q_server, low, ups[0])
    o_own, kv_server = after([o_own, kv_server], [queries])
    o_server = gather_rows(o_own)
    keys_values = rows_matmul(act, kv_server, low, ups[1])
    attended = attend(queries, keys_values, lengths, queries.shape[1] // HS)
    result = columns(o_server, idx, attended, tp_step((attended, attended)), gain_all, mid_own, False)
    result = tp_send(by_xor(result.reshape(tp_count, -1, seq_len)))
    result = finish(idx, result, rows)
    final = final.reshape((1, heads, inner // heads, state_dim))
    state = jnp.where((live > 0)[:, None, None, None], final, incoming_mamba_state)
    return (result[None], state)


def solution(mesh):
    placed = (
        P("req", None, None),
        P("req", None, None),
        P("req"),
        P("req"),
        P("req"),
        P("req", "tp", None, None),
        P(),
        P(("req", "tp"), None, None),
        P(("req", "tp"), None),
        P(None, "tp"),
        P(),
        P("tp"),
        P("tp"),
        P("tp"),
        P("tp"),
        P(None, ("req", "tp")),
        P(),
        P(("req", "tp"), None, None),
        P(),
        P(None, None, None, "tp"),
        P(None, ("req", "tp")),
    )
    return jax.shard_map(
        local,
        mesh=mesh,
        in_specs=placed,
        out_specs=(P("req", None, "tp"), P("req", "tp", None, None)),
        check_vma=False,
    )
```
